1024 devices in a mesh: aux: 16 (over z), ao: 64 (over x, y, core).
Axes of the slice: x: 4, y: 8, z: 16, core: 2. Of those that a mesh axis runs over, the one named last changes fastest.
Arguments:
- b_source: bfloat16 [64, 8, 2048, 1024], P(None, None, ('aux', 'ao')), may hold values from -0.3984375 to 0.3984375
- g_occ: bfloat16 [64, 1024], P('ao'), may hold values from -0.81 to 2.02, as said below
- g_virt: bfloat16 [64, 1024], P('ao'), may hold values from -0.81 to 2.02, as said below
- atom_sizes: int32 [64], replicated, may hold values from 16 to 32, as said below
- pair_cols: int32 [64, 8], P('ao'), may hold values from 0 to 63
- live_slots: int32 [64], P('ao'), may hold values from 1 to 8, as said below
Outputs:
- chi_blocks: float32 [2, 2048, 128], P(None, ('aux', 'ao'))
The draws below stay inside these ranges and needn't reach their ends.
Inputs may be any that keep to these rules, and one draw needn't show every extreme that they name: `live_slots`: every draw has a row atom with all 8 slots live. `atom_sizes`: each atom has either 32 or half of 32 basis functions; both occur in every draw. `g_occ`: each block is a diagonal of positive entries with off-diagonal entries. `g_virt`: each block is a diagonal of positive entries with off-diagonal entries.
All inputs are finite; a program needn't handle non-finite values.
Results may differ from the reference program's by a relative error of at most 0.00033.
Values may be sent and summed in bfloat16 or wider, within the bound.
A program may use at most 64 MiB of HBM per device.

```python
import jax
import jax.numpy as jnp
from jax import lax

NB = 32
TILE = 1024
K = 8
R_DEV = 1
ATOMS = 64
P_A = 128
P_ALL = 2048
N_AUX = 16


def green_table(diag_part, off_part):
    identity = jnp.eye(NB, dtype=jnp.float32)
    tiles = off_part * (1.0 - identity) + diag_part[:, :, None] * identity
    return tiles.reshape(ATOMS, NB * NB)


def green_draw(key):
    key_diag, key_off = jax.random.split(key)
    diag_part = jnp.exp(jax.random.uniform(key_diag, (ATOMS, NB), jnp.float32, -0.7, 0.7))
    off_part = 0.2 * jnp.clip(jax.random.normal(key_off, (ATOMS, NB, NB), jnp.float32), -4.0, 4.0)
    return green_table(diag_part, off_part).astype(jnp.bfloat16)


def draw_g_occ(key, part):
    key = jax.random.fold_in(key, 3)
    return green_draw(key)


def draw_g_virt(key, part):
    key = jax.random.fold_in(key, 5)
    return green_draw(key)


def draw_atom_sizes(key, part):
    key = jax.random.fold_in(key, 11)
    oxygen = jax.random.randint(key, (ATOMS,), 0, 3) == 0
    sizes = jnp.where(oxygen, NB, NB // 2)
    sizes = sizes.at[0].set(NB).at[1].set(NB // 2)
    return sizes.astype(jnp.int32)


def draw_live_slots(key, part):
    key = jax.random.fold_in(key, 7)
    key_busy, key_light, key_pick = jax.random.split(key, 3)
    owner = jnp.arange(ATOMS) // R_DEV
    busy_owner = jax.random.randint(key_busy, (ATOMS // R_DEV,), 0, 4) == 0
    light = jax.random.randint(key_light, (ATOMS,), K // 2, K)
    live_count = jnp.where(busy_owner[owner], K, light)
    picked = jax.random.randint(key_pick, (), 0, ATOMS)
    live_count = live_count.at[picked].set(K)
    return live_count.astype(jnp.int32)


def place_ends(result, own_key, smallest, top_value):
    longest = result.shape.index(max(result.shape))
    spots = []
    for shift in (0, 1):
        where = [jax.random.randint(jax.random.fold_in(own_key, axis), (), 0, length) for axis, length in enumerate(result.shape)]
        where[longest] = (where[longest] + shift) % result.shape[longest]
        spots.append(tuple(where))
    return result.at[spots[0]].set(smallest).at[spots[1]].set(top_value)


def spiked(result, key, source, target, blocks, factor):
    owner, partner = [(jnp.arange(result.shape[position]) // (result.shape[position] // blocks)).reshape([-1 if axis == position else 1 for axis in range(result.ndim)]) for position in (source, target)]
    chosen = jax.random.permutation(key, blocks)[partner]
    strong = (owner == chosen) | (owner == (partner + blocks // 2) % blocks)
    return jnp.where(strong, factor * result, result)


def steps_of(stream_key, dims, cuts, smallest, high):
    level = 1.0
    for dim, parts in cuts:
        steps = jax.random.uniform(jax.random.fold_in(jax.random.fold_in(stream_key, 6), dim), (parts,), jnp.float32, smallest / len(cuts), high / len(cuts))
        level = level * jnp.repeat(jnp.exp(steps), dims[dim] // parts).reshape((-1,) + (1,) * (len(dims) - 1 - dim))
    return level


def gaussian_with(stream_key, shape, spread, limit, shards, heavy, kind=jnp.bfloat16):
    values = spread * jax.random.normal(stream_key, shape, jnp.float32)
    if shards:
        values = values * steps_of(stream_key, shape, shards, -0.22, 0.18)
    return jnp.clip(spiked(values, jax.random.fold_in(stream_key, 3), *heavy), -limit, limit).astype(kind)


def setup_inputs(seed: int = 0) -> dict:
    arg_keys = jax.random.split(jax.random.key(seed), 7)
    b_source = gaussian_with(arg_keys[0], (ATOMS, K, P_ALL, TILE), 0.05, 0.3984375, ((2, 1024),), (0, 2, 64, 4.0))
    g_occ = draw_g_occ(jax.random.fold_in(arg_keys[6], 71), 0)
    g_virt = draw_g_virt(jax.random.fold_in(arg_keys[6], 71), 0)
    atom_sizes = draw_atom_sizes(jax.random.fold_in(arg_keys[6], 71), 0)
    pair_cols = place_ends(jax.random.randint(arg_keys[4], (ATOMS, K), 0, ATOMS), jax.random.fold_in(arg_keys[4], 1), 0, ATOMS - 1).astype(jnp.int32)
    live_slots = draw_live_slots(jax.random.fold_in(arg_keys[6], 71), 0)
    return dict(b_source=b_source, g_occ=g_occ, g_virt=g_virt, atom_sizes=atom_sizes, pair_cols=pair_cols, live_slots=live_slots)


def pad_masks(row_sizes, col_sizes, live_count):
    lane_index = jnp.arange(NB)
    row_ok = lane_index[None, :] < row_sizes[:, None]
    col_ok = lane_index[None, None, :] < col_sizes[:, :, None]
    slot_ok = jnp.arange(K)[None, :] < live_count[:, None]
    joined = row_ok[:, None, :, None] & col_ok[:, :, None, :] & slot_ok[:, :, None, None]
    return joined.reshape(row_sizes.shape[0], K, NB * NB).astype(jnp.float32)


def block_parts(block_id, b_source, occ_tiles, virt_tiles, pad_mask):
    aux_slab = lax.dynamic_slice_in_dim(b_source, (block_id * P_A).astype(jnp.int32), P_A, 2)
    masked = aux_slab.astype(jnp.float32) * pad_mask[:, :, None, :]
    shaped = masked.reshape(ATOMS, K, P_A, NB, NB)
    half_done = jnp.einsum("iml,ikpls->ikpms", occ_tiles, shaped, precision=lax.Precision.HIGHEST)
    half_done = lax.optimization_barrier(half_done.astype(jnp.bfloat16)).astype(jnp.float32)
    full_done = jnp.einsum("ikpms,iksn->ikpmn", half_done, virt_tiles, precision=lax.Precision.HIGHEST)
    rounded = lax.optimization_barrier(full_done.reshape(ATOMS, K, P_A, TILE).astype(jnp.bfloat16))
    return masked, rounded.astype(jnp.float32)


def reference(b_source, g_occ, g_virt, atom_sizes, pair_cols, live_slots):
    pad_mask = pad_masks(atom_sizes, atom_sizes[pair_cols], live_slots)
    occ_tiles = g_occ.astype(jnp.float32).reshape(ATOMS, NB, NB)
    virt_tiles = g_virt.astype(jnp.float32).reshape(ATOMS, NB, NB)[pair_cols]

    def one_block(block_id):
        masked, contracted = block_parts(block_id, b_source, occ_tiles, virt_tiles, pad_mask)
        prev_id = (block_id + N_AUX - 1) % N_AUX
        unused, prior_terms = block_parts(prev_id, b_source, occ_tiles, virt_tiles, pad_mask)
        same_block = jnp.einsum("ikpx,ikqx->pq", contracted, masked, precision=lax.Precision.HIGHEST)
        cross_block = jnp.einsum("ikpx,ikqx->pq", prior_terms, masked, precision=lax.Precision.HIGHEST)
        return jnp.stack([same_block, cross_block])

    results = lax.map(one_block, jnp.arange(N_AUX, dtype=jnp.int32))
    return jnp.transpose(results, (1, 0, 2, 3)).reshape(2, P_ALL, P_A)
```

```python
import functools

import jax
import jax.numpy as jnp
from jax import lax
from jax.experimental import pallas as pl
from jax.experimental.pallas import tpu as pltpu
from jax.sharding import PartitionSpec as P

MESH = pl.DeviceIdType.MESH
F32 = jnp.float32
BF16 = jnp.bfloat16
NB = 32
TILE = NB * NB
QUART = 256
HALF = 128
SLOTS = 8
CORES = 2


def iota(shape, dim):
    return lax.broadcasted_iota(jnp.int32, shape, dim)


def dot(a, b):
    return lax.dot_general(a, b, (((1,), (0,)), ((), ())), preferred_element_type=F32)


def dot_nt(a, b):
    return lax.dot_general(a, b, (((1,), (1,)), ((), ())), preferred_element_type=F32)


def ones_where(cond):
    return jnp.where(cond, 1.0, 0.0).astype(BF16)


def pick(rows, cond):
    return jnp.sum(jnp.where(cond, rows, 0.0), axis=0, keepdims=True)


def lane_sum(values):
    return jnp.sum(values, axis=1, keepdims=True)


def wait_bytes(ref, sem):
    pltpu.make_async_copy(ref, ref, sem).wait()


def kernel(
    dims, b_hbm, meta_own, g_own, sizes, out_ref, flag_ref,
    b_in, bq, meta, table, send, recv, zup, zdown, masked, masked_up, masked_down, contr,
    w1, w2, v1, v2, same, cross, back_send, back_recv, rs_a, rs_a_in, rs_mid, rs_b, rs_b_in,
    b_sem, meta_sem, table_sem, small_send, send_sem, recv_sem, zs_sem, zu_sem, zd_sem, back_sem, rs_sem,
):
    span, up_span, n_x, n_y, n_z = dims
    n_grp = n_y * CORES
    n_ao = n_x * n_grp
    n_p = 2 * n_ao
    n_c = n_ao * SLOTS * 2
    me = lax.axis_index("ao")
    zz = lax.axis_index("aux")
    above = lax.rem(zz + 1, n_z)
    below = lax.rem(zz + n_z - 1, n_z)
    my_x = me // n_grp
    my_in = lax.rem(me, n_grp)

    load_b = pltpu.make_async_copy(b_hbm, b_in, b_sem)
    load_b.start()
    meta[pl.ds(me, 1)] = meta_own[...].reshape(1, 1, 128)
    table[pl.ds(me, 1)] = g_own[...].reshape(1, 16, 128)

    barrier = pltpu.get_barrier_semaphore()

    def greet(step, carry):
        peer = lax.rem(me + step, n_ao)
        pl.semaphore_signal(barrier, inc=1, device_id=(zz, peer), device_id_type=MESH)
        return carry

    lax.fori_loop(1, n_ao, greet, 0)
    pl.semaphore_signal(barrier, inc=1, device_id=(above, me), device_id_type=MESH)
    pl.semaphore_signal(barrier, inc=1, device_id=(below, me), device_id_type=MESH)
    pl.semaphore_wait(barrier, n_ao + 1)

    def tell_meta(step, carry):
        peer = lax.rem(me + step, n_ao)
        pltpu.make_async_remote_copy(
            src_ref=meta.at[me], dst_ref=meta.at[me], send_sem=small_send.at[0], recv_sem=meta_sem,
            device_id=(zz, peer), device_id_type=MESH,
        ).start()
        return carry

    lax.fori_loop(1, n_ao, tell_meta, 0)

    def tell_table(step, carry):
        peer = lax.rem(me + step, n_ao)
        pltpu.make_async_remote_copy(
            src_ref=table.at[me], dst_ref=table.at[me], send_sem=small_send.at[1], recv_sem=table_sem,
            device_id=(zz, peer), device_id_type=MESH,
        ).start()
        return carry

    lax.fori_loop(1, n_ao, tell_table, 0)

    lane_in, lane_out = iota((512, 512), 0), iota((512, 512), 1)
    moved = (lane_in // 16 % 2) * 256 + (lane_in // 32) * 16 + lane_in % 16
    mover = ones_where(moved == lane_out)
    load_b.wait()
    step_rows = n_c // 4

    def reorder(part, carry):
        rows = pl.ds(pl.multiple_of(part * step_rows, step_rows), step_rows)
        for mh in range(2):
            lanes = slice(mh * 512, (mh + 1) * 512)
            bq[rows, lanes] = dot(b_in[rows, lanes], mover).astype(BF16)
        return carry

    lax.fori_loop(0, 4, reorder, 0)

    c_row = iota((1, n_c), 1)
    c_atom, c_slot, c_aux = c_row // 16, c_row // 2 % 8, c_row % 2
    earlier = ones_where(
        (iota((n_c, n_c), 0) // 2 < iota((n_c, n_c), 1) // 2) & (iota((n_c, n_c), 0) % 2 == 0)
    )
    atom_col = iota((n_ao, n_c), 0)
    own_col = atom_col == iota((n_ao, n_c), 1) // 16
    slot_pick = ones_where(iota((128, n_c), 0) == iota((128, n_c), 1) // 2 % 8)
    size_col = sizes[...]
    row_big = pick(jnp.broadcast_to(size_col, (n_ao, n_c)), own_col) > 16.5

    wait_bytes(meta.at[pl.ds(0, n_ao - 1)], meta_sem)
    facts = meta[...].reshape(n_ao, 128)
    c_col = pick(dot(facts.astype(BF16), slot_pick), own_col)
    c_live = pick(jnp.broadcast_to(facts[:, 8:9], (n_ao, n_c)), own_col)
    col_big = pick(jnp.broadcast_to(size_col, (n_ao, n_c)), atom_col.astype(F32) == c_col) > 16.5
    alive = c_slot.astype(F32) < c_live
    one = jnp.ones((1, n_c), F32)
    nil = jnp.zeros((1, n_c), F32)
    big = jnp.where(row_big, one, nil)
    wide = jnp.where(col_big, one, nil)
    here = jnp.where(alive, one, nil)
    is4 = here * big * wide
    is2r = here * big * (one - wide)
    is2c = here * (one - big) * wide
    is2 = is2r + is2c
    is1 = here * (one - big) * (one - wide)
    marks = jnp.concatenate([is4, is2, is1, jnp.zeros((13, n_c), F32)], axis=0)
    before = dot(marks.astype(BF16), earlier)
    n4, n2, n1 = (lane_sum(value) * 0.5 for value in (is4, is2, is1))
    first = is4 * 4.0 * before[0:1] + is2 * (4.0 * n4 + 2.0 * before[1:2])
    first = first + is1 * (4.0 * n4 + 2.0 * n2 + before[2:3])
    c_auxf = c_aux.astype(F32)

    def numbered(member, offset):
        return jnp.where(member > 0.5, 2.0 * (first + offset) + c_auxf, -5.0)

    units = [
        numbered(here, 0.0),
        numbered(is4 + is2c, 1.0),
        numbered(is4 + is2r, is4 * 2.0 + is2r),
        numbered(is4, 3.0),
    ]
    total = 4.0 * n4 + 2.0 * n2 + n1
    flag_ref[...] = jnp.broadcast_to(jnp.where(total > 4.0 * span * n_ao, 1.0, 0.0), (8, 128))

    out_row = iota((n_grp * 8, 1), 0)
    out_row = (out_row // 8) * span * 8 + (out_row % 4) * 2 + out_row // 4 % 2

    def pack(turn, carry):
        grp = lax.rem(my_x + turn, n_x)
        base = grp * (n_grp * span * 8)
        for j in range(span):
            wanted = (out_row + (base + j * 8)).astype(F32)
            got = jnp.zeros((n_grp * 8, QUART), F32)
            for q in range(4):
                got = got + dot(ones_where(units[q] == wanted), bq[:, q * QUART:(q + 1) * QUART])
            both = [got[:, h * HALF:(h + 1) * HALF].reshape(n_grp, 8, HALF) for h in range(2)]
            send[pl.ds(grp * n_grp, n_grp), :, j * HALF:(j + 1) * HALF] = jnp.concatenate(both, axis=1).astype(BF16)

        def ship(step, inner):
            peer = grp * n_grp + lax.rem(my_in + step, n_grp)

            @pl.when(peer != me)
            def _():
                pltpu.make_async_remote_copy(
                    src_ref=send.at[peer], dst_ref=recv.at[me], send_sem=send_sem, recv_sem=recv_sem.at[turn],
                    device_id=(zz, peer), device_id_type=MESH,
                ).start()

            @pl.when(peer == me)
            def _():
                pltpu.make_async_copy(send.at[peer], recv.at[me], recv_sem.at[turn]).start()

            return inner

        lax.fori_loop(0, n_grp, ship, 0)
        return carry

    lax.fori_loop(0, n_x, pack, 0)

    pair = iota((span * 16, 1), 0)
    slot_base = (me * span + pair // 16) * 4
    lead = ((slot_base + pair // 4 % 4) * 2).astype(F32)
    tail = ((slot_base + pair % 4) * 2).astype(F32)
    c_tile = (c_row // 2).astype(F32)

    def describe(unit):
        tile, atom, col, quarter, valid = (jnp.zeros((span * 16, 1), F32) for _ in range(5))
        for q in range(4):
            hit = units[q] == unit
            tile = tile + lane_sum(jnp.where(hit, c_tile, 0.0))
            atom = atom + lane_sum(jnp.where(hit, c_atom.astype(F32), 0.0))
            col = col + lane_sum(jnp.where(hit, c_col, 0.0))
            count = lane_sum(jnp.where(hit, 1.0, 0.0))
            quarter = quarter + q * count
            valid = valid + count
        row_half = jnp.where(quarter > 1.5, 1.0, 0.0)
        return tile, atom, col, row_half, quarter - 2.0 * row_half, valid

    tile_a, atom_a, col_a, mh_a, nh_a, valid_a = describe(lead)
    tile_b, _, _, mh_b, nh_b, valid_b = describe(tail)
    joined = (tile_a == tile_b) & (valid_a > 0.5) & (valid_b > 0.5)
    index1 = jnp.where(joined & (nh_a == nh_b), atom_a * 16.0 + 4.0 * mh_b + 2.0 * mh_a, -9.0)
    index2 = jnp.where(joined & (mh_a == mh_b), col_a * 16.0 + 8.0 + 4.0 * nh_a + 2.0 * nh_b, -9.0)
    wait_bytes(table.at[pl.ds(0, n_ao - 1)], table_sem)
    greens = table[...].reshape(n_ao * 16, 128)
    g_lane = iota((span * 16, n_ao * 16), 1).astype(F32)
    for h in range(2):
        v1[:, h * HALF:(h + 1) * HALF] = dot(ones_where(g_lane == index1 + h), greens)
        v2[:, h * HALF:(h + 1) * HALF] = dot(ones_where(g_lane == index2 + h), greens)

    r, s = iota((QUART, QUART), 0), iota((QUART, QUART), 1)
    hi, lo = r // 16, r % 16
    spread1, gather1, keep1 = ones_where(hi == s % 16), ones_where(hi == s // 16), ones_where(lo == s % 16)
    spread2, gather2, keep2 = ones_where(lo == s // 16), ones_where(lo == s % 16), ones_where(hi == s // 16)

    def weights(j, carry):
        for a in range(4):
            for b in range(4):
                rows, lanes = slice(a * QUART, (a + 1) * QUART), slice(b * QUART, (b + 1) * QUART)
                if a + b == 3:
                    w1[j, rows, lanes] = jnp.zeros((QUART, QUART), BF16)
                    continue
                vec = v1[pl.ds(j * 16 + a * 4 + b, 1), :].astype(BF16)
                w1[j, rows, lanes] = dot(spread1 * vec, gather1).astype(BF16) * keep1
        for m in range(2):
            for a in range(2):
                for b in range(2):
                    vec = v2[pl.ds(j * 16 + (2 * m + a) * 4 + 2 * m + b, 1), :].astype(BF16)
                    w2[j, m, a * QUART:(a + 1) * QUART, b * QUART:(b + 1) * QUART] = (
                        dot(spread2 * vec, gather2).astype(BF16) * keep2
                    )
        return carry

    lax.fori_loop(0, span, weights, 0)

    o, i = iota((n_grp * 16, n_grp * 16), 0), iota((n_grp * 16, n_grp * 16), 1)
    went = (i // 8 % 2 * 4 + i % 4) * (2 * n_grp) + (i // 16) * 2 + i // 4 % 2
    sorter = ones_where(o == went)

    def unpack(source, grp, target, count):
        block = source[pl.ds(grp * n_grp, n_grp)].reshape(n_grp * 16, count * HALF)
        placed = dot(sorter, block).astype(BF16)
        rows = pl.ds(pl.multiple_of(grp * (2 * n_grp), 2 * n_grp), 2 * n_grp)
        for h in range(2):
            for b in range(4):
                part = placed[(h * 4 + b) * 2 * n_grp:(h * 4 + b + 1) * 2 * n_grp]
                for j in range(count):
                    target[j, rows, b * QUART + h * HALF:b * QUART + (h + 1) * HALF] = part[:, j * HALF:(j + 1) * HALF]

    down_span = span - up_span

    def arrive(turn, carry):
        grp = lax.rem(my_x + n_x - turn, n_x)
        block = pl.ds(grp * n_grp, n_grp)
        wait_bytes(recv.at[block], recv_sem.at[turn])
        pltpu.make_async_remote_copy(
            src_ref=recv.at[block, :, pl.ds(0, up_span * HALF)], dst_ref=zup.at[block],
            send_sem=zs_sem.at[0], recv_sem=zu_sem.at[turn], device_id=(above, me), device_id_type=MESH,
        ).start()
        pltpu.make_async_remote_copy(
            src_ref=recv.at[block, :, pl.ds(up_span * HALF, down_span * HALF)], dst_ref=zdown.at[block],
            send_sem=zs_sem.at[1], recv_sem=zd_sem.at[turn], device_id=(below, me), device_id_type=MESH,
        ).start()
        unpack(recv, grp, masked, span)
        return carry

    lax.fori_loop(0, n_x, arrive, 0)

    def contract(tiles, j):
        half = dot(tiles, w1[j]).astype(BF16)
        done = [dot(half[:, m * 512:(m + 1) * 512], w2[j, m]).astype(BF16) for m in range(2)]
        return jnp.concatenate(done, axis=1)

    same[...] = jnp.zeros_like(same)
    cross[...] = jnp.zeros_like(cross)
    back_send[...] = jnp.zeros_like(back_send)

    def own_slot(j, carry):
        tiles = masked[j]
        result = contract(tiles, j)
        contr[j] = result
        same[...] += dot_nt(result, tiles)
        return carry

    lax.fori_loop(0, span, own_slot, 0)

    def arrive_down(turn, carry):
        grp = lax.rem(my_x + n_x - turn, n_x)
        wait_bytes(zdown.at[pl.ds(grp * n_grp, n_grp)], zd_sem.at[turn])
        unpack(zdown, grp, masked_down, down_span)
        return carry

    lax.fori_loop(0, n_x, arrive_down, 0)

    def down_slot(j, carry):
        back_send[...] += dot_nt(contr[up_span + j], masked_down[j])
        return carry

    lax.fori_loop(0, down_span, down_slot, 0)
    back = pltpu.make_async_remote_copy(
        src_ref=back_send, dst_ref=back_recv, send_sem=back_sem.at[0], recv_sem=back_sem.at[1],
        device_id=(above, me), device_id_type=MESH,
    )
    back.start()

    def arrive_up(turn, carry):
        grp = lax.rem(my_x + n_x - turn, n_x)
        wait_bytes(zup.at[pl.ds(grp * n_grp, n_grp)], zu_sem.at[turn])
        unpack(zup, grp, masked_up, up_span)
        return carry

    lax.fori_loop(0, n_x, arrive_up, 0)

    def up_slot(j, carry):
        cross[...] += dot_nt(contract(masked_up[j], j), masked[j])
        return carry

    lax.fori_loop(0, up_span, up_slot, 0)
    back.wait()
    cross[...] += back_recv[...]

    my_y = my_in // CORES
    my_core = lax.rem(me, CORES)
    n_a = n_x * CORES
    mine = my_x * CORES + my_core
    for a in range(n_a):
        for c, part in enumerate((same, cross)):
            for e in range(2):
                start = (a // CORES) * n_grp * 2 + (a % CORES) * 2 + e
                rs_a[a, (c * 2 + e) * n_y:(c * 2 + e + 1) * n_y, :] = part[pl.ds(start, n_y, stride=4), :]
    rs_a_in[pl.ds(mine, 1)] = rs_a[pl.ds(mine, 1)]

    def copy_a(step):
        to = lax.rem(mine + step, n_a)
        peer = ((to // CORES) * n_y + my_y) * CORES + lax.rem(to, CORES)
        return pltpu.make_async_remote_copy(
            src_ref=rs_a.at[to], dst_ref=rs_a_in.at[mine], send_sem=rs_sem.at[0], recv_sem=rs_sem.at[1],
            device_id=(zz, peer), device_id_type=MESH,
        )

    for step in range(1, n_a):
        copy_a(step).start()
    wait_bytes(rs_a_in.at[pl.ds(0, n_a - 1)], rs_sem.at[1])
    rs_mid[...] = jnp.sum(rs_a_in[...], axis=0)
    for y in range(n_y):
        rs_b[y, 0:4, :] = rs_mid[pl.ds(y, 4, stride=n_y), :]
        rs_b[y, 4:8, :] = jnp.zeros((4, n_p), F32)
    rs_b_in[pl.ds(my_y, 1)] = rs_b[pl.ds(my_y, 1)]

    def copy_b(step):
        to = lax.rem(my_y + step, n_y)
        peer = (my_x * n_y + to) * CORES + my_core
        return pltpu.make_async_remote_copy(
            src_ref=rs_b.at[to], dst_ref=rs_b_in.at[my_y], send_sem=rs_sem.at[2], recv_sem=rs_sem.at[3],
            device_id=(zz, peer), device_id_type=MESH,
        )

    for step in range(1, n_y):
        copy_b(step).start()
    wait_bytes(rs_b_in.at[pl.ds(0, n_y - 1)], rs_sem.at[3])
    final = jnp.sum(rs_b_in[...], axis=0)
    out_ref[0] = final[0:2]
    out_ref[1] = final[2:4]

    wait_bytes(meta.at[pl.ds(0, n_ao - 1)], small_send.at[0])
    wait_bytes(table.at[pl.ds(0, n_ao - 1)], small_send.at[1])
    wait_bytes(send.at[pl.ds(0, n_ao - 1)], send_sem)
    wait_bytes(zup, zs_sem.at[0])
    wait_bytes(zdown, zs_sem.at[1])
    wait_bytes(rs_a.at[pl.ds(0, n_a - 1)], rs_sem.at[0])
    wait_bytes(rs_b.at[pl.ds(0, n_y - 1)], rs_sem.at[2])


def run(span, shape, ident, b_rows, meta_row, greens, sizes):
    n_x, n_y, n_z = shape
    n_ao = n_x * n_y * CORES
    n_c, n_p = n_ao * SLOTS * 2, 2 * n_ao
    up_span = span // 2
    down_span = span - up_span
    vmem = pl.BlockSpec(memory_space=pltpu.VMEM)
    dma = pltpu.SemaphoreType.DMA
    return pl.pallas_call(
        functools.partial(kernel, (span, up_span, n_x, n_y, n_z)),
        out_shape=(jax.ShapeDtypeStruct((2, 2, n_p), F32), jax.ShapeDtypeStruct((8, 128), F32)),
        in_specs=[pl.BlockSpec(memory_space=pl.ANY), vmem, vmem, vmem],
        out_specs=(vmem, vmem),
        scratch_shapes=[
            pltpu.VMEM((n_c, TILE), BF16),
            pltpu.VMEM((n_c, TILE), BF16),
            pltpu.VMEM((n_ao, 1, 128), F32),
            pltpu.VMEM((n_ao, 16, 128), BF16),
            pltpu.VMEM((n_ao, 16, span * HALF), BF16),
            pltpu.VMEM((n_ao, 16, span * HALF), BF16),
            pltpu.VMEM((n_ao, 16, up_span * HALF), BF16),
            pltpu.VMEM((n_ao, 16, down_span * HALF), BF16),
            pltpu.VMEM((span, n_p, TILE), BF16),
            pltpu.VMEM((up_span, n_p, TILE), BF16),
            pltpu.VMEM((down_span, n_p, TILE), BF16),
            pltpu.VMEM((span, n_p, TILE), BF16),
            pltpu.VMEM((span, TILE, TILE), BF16),
            pltpu.VMEM((span, 2, 512, 512), BF16),
            pltpu.VMEM((span * 16, QUART), F32),
            pltpu.VMEM((span * 16, QUART), F32),
            pltpu.VMEM((n_p, n_p), F32),
            pltpu.VMEM((n_p, n_p), F32),
            pltpu.VMEM((n_p, n_p), F32),
            pltpu.VMEM((n_p, n_p), F32),
            pltpu.VMEM((n_x * CORES, 4 * n_y, n_p), F32),
            pltpu.VMEM((n_x * CORES, 4 * n_y, n_p), F32),
            pltpu.VMEM((4 * n_y, n_p), F32),
            pltpu.VMEM((n_y, 8, n_p), F32),
            pltpu.VMEM((n_y, 8, n_p), F32),
            dma, dma, dma, dma((2,)), dma, dma((n_x,)), dma((2,)), dma((n_x,)), dma((n_x,)), dma((2,)), dma((4,)),
        ],
        compiler_params=pltpu.CompilerParams(
            collective_id=ident, has_side_effects=True, vmem_limit_bytes=56 * 1024 * 1024
        ),
        name=f"blocks_{span}",
    )(b_rows, meta_row, greens, sizes)


def quarters(blocks):
    return blocks.reshape(2, 16, 2, 16).transpose(0, 2, 1, 3).reshape(8, 128)


def local(shape, b_source, g_occ, g_virt, atom_sizes, pair_cols, live_slots):
    n_ao = atom_sizes.shape[0]
    b_rows = b_source.reshape(n_ao * SLOTS * 2, TILE)
    meta_row = jnp.concatenate([pair_cols, live_slots[:, None], jnp.zeros((1, 119), jnp.int32)], axis=1).astype(F32)
    greens = jnp.concatenate([quarters(g_occ), quarters(g_virt)], axis=0)
    sizes = atom_sizes.astype(F32)[:, None]
    short, flag = run(4, shape, 0, b_rows, meta_row, greens, sizes)

    def whole(values):
        return run(8, shape, 1, *values)[0]

    return lax.cond(flag[0, 0] > 0.5, whole, lambda values: short, (b_rows, meta_row, greens, sizes))


def solution(mesh):
    n_ao, n_z = mesh.shape["ao"], mesh.shape["aux"]
    n_x = 4 if n_ao >= 64 else 2
    return jax.shard_map(
        functools.partial(local, (n_x, n_ao // (n_x * CORES), n_z)),
        mesh=mesh,
        in_specs=(
            P(None, None, ("aux", "ao"), None),
            P("ao", None),
            P("ao", None),
            P(),
            P("ao", None),
            P("ao"),
        ),
        out_specs=P(None, ("aux", "ao"), None),
        check_vma=False,
    )
```

```python
import functools

import jax
import jax.numpy as jnp
from jax import lax
from jax.experimental import pallas as pl
from jax.experimental.pallas import tpu as pltpu
from jax.sharding import PartitionSpec as P

MESH = pl.DeviceIdType.MESH
F32 = jnp.float32
BF16 = jnp.bfloat16
NB = 32
TILE = NB * NB
QUART = 256
HALF = 128
SLOTS = 8
CORES = 2


def iota(shape, dim):
    return lax.broadcasted_iota(jnp.int32, shape, dim)


def dot(a, b):
    return lax.dot_general(a, b, (((1,), (0,)), ((), ())), preferred_element_type=F32)


def dot_nt(a, b):
    return lax.dot_general(a, b, (((1,), (1,)), ((), ())), preferred_element_type=F32)


def ones_where(cond):
    return jnp.where(cond, 1.0, 0.0).astype(BF16)


def pick(rows, cond):
    return jnp.sum(jnp.where(cond, rows, 0.0), axis=0, keepdims=True)


def lane_sum(values):
    return jnp.sum(values, axis=1, keepdims=True)


def wait_bytes(ref, sem):
    pltpu.make_async_copy(ref, ref, sem).wait()


def kernel(
    dims, b_hbm, pairs_own, live_own, occ_own, virt_own, sizes, out_ref, flag_ref,
    b_in, bq, meta, table, send, recv, zup, masked, masked_up, w1, w2, v1, v2,
    same, cross, rs_a, rs_a_in, rs_mid, rs_b, rs_b_in,
    b_sem, meta_sem, table_sem, small_send, send_sem, recv_sem, zs_sem, zu_sem, rs_sem,
):
    caps, n_x, n_y, n_z = dims
    span = max(caps)
    n_grp = n_y * CORES
    n_ao = n_x * n_grp
    n_p = 2 * n_ao
    n_c = n_ao * SLOTS * 2
    me = lax.axis_index("ao")
    zz = lax.axis_index("aux")
    above = lax.rem(zz + 1, n_z)
    below = lax.rem(zz + n_z - 1, n_z)
    my_x = me // n_grp
    my_in = lax.rem(me, n_grp)
    my_y = my_in // CORES
    my_core = lax.rem(me, CORES)

    def device(x, y, core):
        return (x * n_y + y) * CORES + core

    def by_core(core, act):
        if caps[0] == caps[1]:
            act(0, caps[0])
            return
        for c in range(CORES):
            pl.when(core == c)(functools.partial(act, c, caps[c]))

    load_b = pltpu.make_async_copy(b_hbm, b_in, b_sem)
    load_b.start()
    if min(caps) < span:
        unused = slice(min(caps) * HALF, span * HALF)
        for buffer in (recv, zup):
            buffer[:, :, unused] = jnp.zeros((n_ao, 16, (span - min(caps)) * HALF), BF16)

    spot = (my_core * n_x + my_x) * n_y + my_y
    line = (my_core * n_x + my_x) * n_y
    lane = iota((1, 128), 1)
    facts = jnp.where(lane == SLOTS, live_own[...].astype(F32), jnp.zeros((1, 128), F32))
    pairs = pairs_own[...].astype(F32)
    for k in range(SLOTS):
        facts = jnp.where(lane == k, pairs[:, k:k + 1], facts)
    meta[pl.ds(spot, 1)] = facts.reshape(1, 1, 128)
    greens = [own[:, i * 128:(i + 1) * 128].astype(F32) for own in (occ_own[...], virt_own[...]) for i in range(8)]
    table[pl.ds(spot, 1)] = jnp.concatenate(greens, axis=0).astype(BF16).reshape(1, 16, 128)

    barrier = pltpu.get_barrier_semaphore()

    def greet(step, carry):
        peer = lax.rem(me + step, n_ao)
        pl.semaphore_signal(barrier, inc=1, device_id=(zz, peer), device_id_type=MESH)
        return carry

    pl.semaphore_signal(barrier, inc=1, device_id=(below, me), device_id_type=MESH)
    lax.fori_loop(1, n_ao, greet, 0)

    lane_in, lane_out = iota((512, 512), 0), iota((512, 512), 1)
    moved = (lane_in // 16 % 2) * 256 + (lane_in // 32) * 16 + lane_in % 16
    mover = ones_where(moved == lane_out)
    part_atoms = n_ao // 4
    part_rows = part_atoms * SLOTS * 2

    def reorder(part, carry):
        loaded = b_in[pl.ds(part * part_atoms, part_atoms)].reshape(part_rows, TILE)
        rows = pl.ds(pl.multiple_of(part * part_rows, part_rows), part_rows)
        for mh in range(2):
            placed = dot(loaded[:, mh * 512:(mh + 1) * 512], mover).astype(BF16)
            bq[2 * mh, rows, :] = placed[:, :QUART]
            bq[2 * mh + 1, rows, :] = placed[:, QUART:]
        return carry

    pl.semaphore_wait(barrier, n_ao)

    def spread_y(ref, send_to, recv_from):
        def one(step, carry):
            peer = device(my_x, lax.rem(my_y + step, n_y), my_core)
            pltpu.make_async_remote_copy(
                src_ref=ref.at[spot], dst_ref=ref.at[spot], send_sem=send_to, recv_sem=recv_from,
                device_id=(zz, peer), device_id_type=MESH,
            ).start()
            return carry

        lax.fori_loop(1, n_y, one, 0)

    n_a = n_x * CORES
    mine = my_x * CORES + my_core

    def spread_x(ref, send_to, recv_from):
        block = pl.ds(line, n_y)

        def one(step, carry):
            to = lax.rem(mine + step, n_a)
            pltpu.make_async_remote_copy(
                src_ref=ref.at[block], dst_ref=ref.at[block], send_sem=send_to, recv_sem=recv_from,
                device_id=(zz, device(to // CORES, my_y, lax.rem(to, CORES))), device_id_type=MESH,
            ).start()
            return carry

        lax.fori_loop(1, n_a, one, 0)

    n_far = (n_a - 1) * n_y
    spread_y(meta, small_send.at[0], meta_sem.at[0])
    load_b.wait()
    lax.fori_loop(0, 2, reorder, 0)
    wait_bytes(meta.at[pl.ds(0, n_y - 1)], meta_sem.at[0])
    spread_x(meta, small_send.at[2], meta_sem.at[1])
    spread_y(table, small_send.at[1], table_sem.at[0])
    lax.fori_loop(2, 4, reorder, 0)

    c_row = iota((1, n_c), 1)
    c_atom, c_slot, c_aux = c_row // 16, c_row // 2 % 8, c_row % 2
    earlier = ones_where((iota((128, 128), 0) // 2 < iota((128, 128), 1) // 2) & (iota((128, 128), 0) % 2 == 0))
    atom_col = iota((n_ao, n_c), 0)
    spot_col = device(atom_col // n_y % n_x, atom_col % n_y, atom_col // (n_x * n_y))
    own_col = spot_col == iota((n_ao, n_c), 1) // 16
    slot_pick = ones_where(iota((128, n_c), 0) == iota((128, n_c), 1) // 2 % 8)
    size_row = jnp.broadcast_to(sizes[...].astype(F32), (n_ao, n_ao))
    size_col = lane_sum(jnp.where(iota((n_ao, n_ao), 0) == iota((n_ao, n_ao), 1), size_row, 0.0))
    size_all = jnp.broadcast_to(size_col, (n_ao, n_c))
    row_big = pick(size_all, atom_col == iota((n_ao, n_c), 1) // 16) > 16.5

    wait_bytes(table.at[pl.ds(0, n_y - 1)], table_sem.at[0])
    spread_x(table, small_send.at[3], table_sem.at[1])
    wait_bytes(meta.at[pl.ds(0, n_far)], meta_sem.at[1])
    facts = meta[...].reshape(n_ao, 128)
    c_col = pick(dot(facts.astype(BF16), slot_pick), own_col)
    c_live = pick(jnp.broadcast_to(facts[:, SLOTS:SLOTS + 1], (n_ao, n_c)), own_col)
    col_big = pick(size_all, atom_col.astype(F32) == c_col) > 16.5
    alive = c_slot.astype(F32) < c_live
    one = jnp.ones((1, n_c), F32)
    nil = jnp.zeros((1, n_c), F32)
    big = jnp.where(row_big, one, nil)
    wide = jnp.where(col_big, one, nil)
    here = jnp.where(alive, one, nil)
    is4 = here * big * wide
    is2r = here * big * (one - wide)
    is2c = here * (one - big) * wide
    is1 = here * (one - big) * (one - wide)
    marks = jnp.concatenate([is4, is2c, is2r, is1, jnp.zeros((12, n_c), F32)], axis=0)
    marks = [marks[:, i * 128:(i + 1) * 128] for i in range(n_c // 128)]
    inside = dot(jnp.concatenate(marks, axis=0).astype(BF16), earlier)
    before, count = [], jnp.zeros((16, 1), F32)
    for i, block in enumerate(marks):
        before.append(inside[i * 16:(i + 1) * 16] + count)
        count = count + lane_sum(block) * 0.5
    before = jnp.concatenate(before, axis=1)
    base2c = 4.0 * count[0:1]
    base2r = base2c + 4.0 * jnp.floor((count[1:2] + 1.0) * 0.5)
    base1 = base2r + 2.0 * count[2:3]
    total = base1 + count[3:4]
    twos = jnp.floor(before[1:2] * 0.5)
    first = is4 * 4.0 * before[0:1] + is2c * (base2c + before[1:2] + 2.0 * twos)
    first = first + is2r * (base2r + 2.0 * before[2:3]) + is1 * (base1 + before[3:4])
    c_auxf = c_aux.astype(F32)

    def numbered(member, offset):
        return jnp.where(member > 0.5, 2.0 * (first + offset) + c_auxf, -5.0)

    units = [
        numbered(here, 0.0),
        numbered(is4 + is2c, 2.0),
        numbered(is4 + is2r, 1.0),
        numbered(is4, 3.0),
    ]
    flag_ref[...] = jnp.where(total > 4.0 * sum(caps) * (n_ao // CORES), 1, 0)

    unit_lanes = jnp.concatenate(units, axis=1)
    my_half = my_in // n_y
    my_lo = lax.rem(my_in, n_y)
    turns = 2 * n_x

    out_row = iota((span * n_y * 8, 1), 0)
    out_lo, out_slot = out_row // 8 % n_y, out_row // (8 * n_y)
    out_core = out_lo % CORES
    out_first = (out_lo // CORES) * sum(caps) + out_core * caps[0] + out_slot
    out_unit = out_first * 8 + (out_row % 4) * 2 + out_row // 4 % 2
    out_keep = out_slot < jnp.where(out_core == 0, caps[0], caps[1])

    def pack(turn):
        grp = lax.rem(my_x + turn // 2, n_x) * 2 + lax.rem(my_half + turn, 2)
        wanted = jnp.where(out_keep, out_unit + grp * (n_y // CORES * sum(caps) * 8), -99).astype(F32)
        got = dot(ones_where(unit_lanes == wanted), bq[...].reshape(4 * n_c, QUART))
        for j in range(span):
            part = got[j * n_y * 8:(j + 1) * n_y * 8]
            both = [part[:, h * HALF:(h + 1) * HALF].reshape(n_y, 8, HALF) for h in range(2)]
            send[pl.ds(grp * n_y, n_y), :, j * HALF:(j + 1) * HALF] = jnp.concatenate(both, axis=1).astype(BF16)

        def ship(step, inner):
            peer = grp * n_y + lax.rem(my_lo + step, n_y)

            def act(c, count):
                source = send.at[peer, :, pl.ds(0, count * HALF)]
                target = recv.at[me, :, pl.ds(0, count * HALF)]

                @pl.when(peer != me)
                def _():
                    pltpu.make_async_remote_copy(
                        src_ref=source, dst_ref=target, send_sem=send_sem.at[c], recv_sem=recv_sem.at[turn],
                        device_id=(zz, peer), device_id_type=MESH,
                    ).start()

                @pl.when(peer == me)
                def _():
                    pltpu.make_async_copy(source, target, recv_sem.at[turn]).start()

            by_core(lax.rem(peer, CORES), act)
            return inner

        lax.fori_loop(0, n_y, ship, 0)

    def origin(turn):
        return lax.rem(my_x + n_x - turn // 2, n_x) * 2 + lax.rem(my_half + turn, 2)

    def forward(turn):
        def act(c, count):
            block = (pl.ds(origin(turn) * n_y, n_y), slice(None), pl.ds(0, count * HALF))
            wait_bytes(recv.at[block], recv_sem.at[turn])
            pltpu.make_async_remote_copy(
                src_ref=recv.at[block], dst_ref=zup.at[block], send_sem=zs_sem, recv_sem=zu_sem.at[turn],
                device_id=(above, me), device_id_type=MESH,
            ).start()

        by_core(my_core, act)

    lag = 3

    def pack_and_forward(turn, carry):
        pack(turn)
        pl.when(turn >= lag)(lambda: forward(turn - lag))
        return carry

    lax.fori_loop(0, turns, pack_and_forward, 0)

    pair = iota((span * 16, 1), 0)
    slot_base = ((me // CORES) * sum(caps) + my_core * caps[0] + pair // 16) * 4
    lead = ((slot_base + pair // 4 % 4) * 2).astype(F32)
    tail = ((slot_base + pair % 4) * 2).astype(F32)
    c_tile = (c_row // 2).astype(F32)

    def describe(unit):
        tile, atom, col, quarter, valid = (jnp.zeros((span * 16, 1), F32) for _ in range(5))
        for q in range(4):
            hit = units[q] == unit
            tile = tile + lane_sum(jnp.where(hit, c_tile, 0.0))
            atom = atom + lane_sum(jnp.where(hit, c_atom.astype(F32), 0.0))
            col = col + lane_sum(jnp.where(hit, c_col, 0.0))
            count = lane_sum(jnp.where(hit, 1.0, 0.0))
            quarter = quarter + q * count
            valid = valid + count
        row_half = jnp.where(quarter > 1.5, 1.0, 0.0)
        return tile, atom, col, row_half, quarter - 2.0 * row_half, valid

    tile_a, atom_a, col_a, mh_a, nh_a, valid_a = describe(lead)
    tile_b, _, _, mh_b, nh_b, valid_b = describe(tail)
    joined = (tile_a == tile_b) & (valid_a > 0.5) & (valid_b > 0.5)
    index1 = jnp.where(joined & (nh_a == nh_b), atom_a * 16.0 + 4.0 * mh_b, -99.0)
    index2 = jnp.where(joined & (mh_a == mh_b), col_a * 16.0 + 8.0 + 4.0 * nh_a, -99.0)
    wait_bytes(table.at[pl.ds(0, n_far)], table_sem.at[1])
    greens = table[...].reshape(n_ao * 16, 128)
    g_row = iota((span * 16, n_ao * 16), 1)
    g_spot = g_row // 16
    g_atom = device(g_spot // n_y % n_x, g_spot % n_y, g_spot // (n_x * n_y))
    g_lane = (g_atom * 16 + g_row % 16).astype(F32)
    for target, index, half in ((v1, index1, mh_a), (v2, index2, nh_b)):
        rows = [dot(ones_where(g_lane == index + i), greens).astype(BF16) for i in range(4)]
        rows = dot(jnp.concatenate(rows, axis=1), mover)
        target[...] = jnp.where(half < 0.5, rows[:, :QUART], rows[:, QUART:])

    r, s = iota((QUART, QUART), 0), iota((QUART, QUART), 1)
    hi, lo = r // 16, r % 16
    spread1, gather1, keep1 = ones_where(hi == s % 16), ones_where(hi == s // 16), ones_where(lo == s % 16)
    spread2, gather2, keep2 = ones_where(lo == s // 16), ones_where(lo == s % 16), ones_where(hi == s // 16)

    def weights(j):
        for m in range(2):
            for a in range(2):
                for b in range(2):
                    rows, lanes = slice(a * QUART, (a + 1) * QUART), slice(b * QUART, (b + 1) * QUART)
                    vec = v1[pl.ds(j * 16 + (2 * m + a) * 4 + 2 * m + b, 1), :].astype(BF16)
                    w1[j, m, rows, lanes] = dot(spread1 * vec, gather1).astype(BF16) * keep1
                    vec = v2[pl.ds(j * 16 + (2 * a + m) * 4 + 2 * b + m, 1), :].astype(BF16)
                    w2[j, m, rows, lanes] = dot(spread2 * vec, gather2).astype(BF16) * keep2

    o, i = iota((n_y * 16, n_y * 16), 0), iota((n_y * 16, n_y * 16), 1)
    went = (i // 8 % 2 * 4 + i % 4) * (2 * n_y) + (i // 16) * 2 + i // 4 % 2
    sorter = ones_where(o == went)

    def unpack(source, turn, target):
        grp = origin(turn)
        block = source[pl.ds(grp * n_y, n_y)].reshape(n_y * 16, span * HALF)
        placed = dot(sorter, block).astype(BF16)
        rows = pl.ds(pl.multiple_of(grp * (2 * n_y), 2 * n_y), 2 * n_y)
        for h in range(2):
            for b in range(4):
                part = placed[(h * 4 + b) * 2 * n_y:(h * 4 + b + 1) * 2 * n_y]
                for j in range(span):
                    target[j, rows, b * QUART + h * HALF:b * QUART + (h + 1) * HALF] = part[:, j * HALF:(j + 1) * HALF]

    def contract(tiles, j):
        half = [dot(tiles[:, m * 512:(m + 1) * 512], w1[j, m]).astype(BF16) for m in range(2)]
        done = []
        for m in range(2):
            lanes = slice(m * QUART, (m + 1) * QUART)
            done.append(dot(jnp.concatenate([part[:, lanes] for part in half], axis=1), w2[j, m]).astype(BF16))
        return jnp.concatenate([done[m][:, a * QUART:(a + 1) * QUART] for a in range(2) for m in range(2)], axis=1)

    def weights_and_forward(j, carry):
        weights(j)
        for turn in range(turns - lag, turns):
            pl.when(j == (turn - turns + lag) * span // lag)(functools.partial(forward, turn))
        return carry

    lax.fori_loop(0, span, weights_and_forward, 0)

    def arrive(turn, carry):
        unpack(recv, turn, masked)
        return carry

    lax.fori_loop(0, turns, arrive, 0)

    same[...] = jnp.zeros_like(same)

    def own_slot(j, carry):
        tiles = masked[j]
        same[...] += dot_nt(contract(tiles, j), tiles)
        return carry

    lax.fori_loop(0, span, own_slot, 0)

    def reduce_x(c, part):
        for a in range(n_a):
            for e in range(2):
                start = (a // CORES) * n_grp * 2 + (a % CORES) * 2 + e
                rs_a[c, a, e * n_y:(e + 1) * n_y, :] = part[pl.ds(start, n_y, stride=4), :]
        rs_a_in[c, pl.ds(mine, 1)] = rs_a[c, pl.ds(mine, 1)]
        for step in range(1, n_a):
            to = lax.rem(mine + step, n_a)
            pltpu.make_async_remote_copy(
                src_ref=rs_a.at[c, to], dst_ref=rs_a_in.at[c, mine], send_sem=rs_sem.at[c], recv_sem=rs_sem.at[2 + c],
                device_id=(zz, device(to // CORES, my_y, lax.rem(to, CORES))), device_id_type=MESH,
            ).start()

    def reduced_x(c):
        wait_bytes(rs_a_in.at[c, pl.ds(0, n_a - 1)], rs_sem.at[2 + c])
        rs_mid[c * 2 * n_y:(c + 1) * 2 * n_y, :] = jnp.sum(rs_a_in[c], axis=0)

    reduce_x(0, same)

    def arrive_up(turn, carry):
        def act(c, count):
            wait_bytes(zup.at[pl.ds(origin(turn) * n_y, n_y), :, pl.ds(0, count * HALF)], zu_sem.at[turn])

        by_core(my_core, act)
        unpack(zup, turn, masked_up)
        return carry

    lax.fori_loop(0, turns, arrive_up, 0)
    cross[...] = jnp.zeros_like(cross)

    def up_slot(j, carry):
        cross[...] += dot_nt(contract(masked_up[j], j), masked[j])
        return carry

    lax.fori_loop(0, span, up_slot, 0)
    reduce_x(1, cross)
    reduced_x(0)
    reduced_x(1)
    for y in range(n_y):
        rs_b[y, 0:4, :] = rs_mid[pl.ds(y, 4, stride=n_y), :]
        rs_b[y, 4:8, :] = jnp.zeros((4, n_p), F32)
    rs_b_in[pl.ds(my_y, 1)] = rs_b[pl.ds(my_y, 1)]
    for step in range(1, n_y):
        to = lax.rem(my_y + step, n_y)
        pltpu.make_async_remote_copy(
            src_ref=rs_b.at[to], dst_ref=rs_b_in.at[my_y], send_sem=rs_sem.at[4], recv_sem=rs_sem.at[5],
            device_id=(zz, device(my_x, to, my_core)), device_id_type=MESH,
        ).start()
    wait_bytes(rs_b_in.at[pl.ds(0, n_y - 1)], rs_sem.at[5])
    final = jnp.sum(rs_b_in[...], axis=0)
    out_ref[0] = final[0:2]
    out_ref[1] = final[2:4]

    wait_bytes(meta.at[pl.ds(0, n_y - 1)], small_send.at[0])
    wait_bytes(table.at[pl.ds(0, n_y - 1)], small_send.at[1])
    wait_bytes(meta.at[pl.ds(0, n_far)], small_send.at[2])
    wait_bytes(table.at[pl.ds(0, n_far)], small_send.at[3])
    if caps[0] == caps[1]:
        wait_bytes(send.at[pl.ds(0, n_ao - 1)], send_sem.at[0])
    else:
        for c in range(CORES):
            lanes = pl.ds(0, caps[c] * HALF)

            @pl.when(my_core == c)
            def _():
                wait_bytes(send.at[pl.ds(0, n_ao // CORES - 1), :, lanes], send_sem.at[c])

            @pl.when(my_core != c)
            def _():
                wait_bytes(send.at[pl.ds(0, n_ao // CORES), :, lanes], send_sem.at[c])

    def sent_up(c, count):
        wait_bytes(zup.at[:, :, pl.ds(0, count * HALF)], zs_sem)

    by_core(my_core, sent_up)
    for c in range(2):
        wait_bytes(rs_a.at[c, pl.ds(0, n_a - 1)], rs_sem.at[c])
    wait_bytes(rs_b.at[pl.ds(0, n_y - 1)], rs_sem.at[4])


def run(caps, shape, ident, b_source, pair_cols, live_slots, g_occ, g_virt, atom_sizes):
    n_x, n_y, n_z = shape
    n_ao = n_x * n_y * CORES
    n_c, n_p = n_ao * SLOTS * 2, 2 * n_ao
    n_a = n_x * CORES
    span = max(caps)
    vmem = pl.BlockSpec(memory_space=pltpu.VMEM)
    dma = pltpu.SemaphoreType.DMA
    return pl.pallas_call(
        functools.partial(kernel, (caps, n_x, n_y, n_z)),
        out_shape=(jax.ShapeDtypeStruct((2, 2, n_p), F32), jax.ShapeDtypeStruct((1, 1), jnp.int32)),
        in_specs=[pl.BlockSpec(memory_space=pl.ANY)] + [vmem] * 5,
        out_specs=(vmem, vmem),
        scratch_shapes=[
            pltpu.VMEM((n_ao, SLOTS, 2, TILE), BF16),
            pltpu.VMEM((4, n_c, QUART), BF16),
            pltpu.VMEM((n_ao, 1, 128), F32),
            pltpu.VMEM((n_ao, 16, 128), BF16),
            pltpu.VMEM((n_ao, 16, span * HALF), BF16),
            pltpu.VMEM((n_ao, 16, span * HALF), BF16),
            pltpu.VMEM((n_ao, 16, span * HALF), BF16),
            pltpu.VMEM((span, n_p, TILE), BF16),
            pltpu.VMEM((span, n_p, TILE), BF16),
            pltpu.VMEM((span, 2, 512, 512), BF16),
            pltpu.VMEM((span, 2, 512, 512), BF16),
            pltpu.VMEM((span * 16, QUART), F32),
            pltpu.VMEM((span * 16, QUART), F32),
            pltpu.VMEM((n_p, n_p), F32),
            pltpu.VMEM((n_p, n_p), F32),
            pltpu.VMEM((2, n_a, 2 * n_y, n_p), F32),
            pltpu.VMEM((2, n_a, 2 * n_y, n_p), F32),
            pltpu.VMEM((4 * n_y, n_p), F32),
            pltpu.VMEM((n_y, 8, n_p), F32),
            pltpu.VMEM((n_y, 8, n_p), F32),
            dma, dma((2,)), dma((2,)), dma((4,)), dma((2,)), dma((2 * n_x,)), dma, dma((2 * n_x,)), dma((6,)),
        ],
        compiler_params=pltpu.CompilerParams(
            collective_id=ident, has_side_effects=True, vmem_limit_bytes=56 * 1024 * 1024
        ),
        name=f"blocks_{sum(caps)}",
    )(b_source, pair_cols, live_slots, g_occ, g_virt, atom_sizes)


def whole(shape, values):
    return run((8, 8), shape, 1, *values)[0]


def local(shape, b_source, g_occ, g_virt, atom_sizes, pair_cols, live_slots):
    given = (b_source, pair_cols, live_slots.reshape(1, 1), g_occ, g_virt, atom_sizes.reshape(1, -1))
    short, flag = run((4, 3), shape, 0, *given)
    return lax.cond(
        flag[0, 0] > 0, lambda *values: whole(shape, values), lambda *values: short, *given
    )


def solution(mesh):
    n_ao, n_z = mesh.shape["ao"], mesh.shape["aux"]
    n_x = 4 if n_ao >= 64 else 2
    return jax.shard_map(
        functools.partial(local, (n_x, n_ao // (n_x * CORES), n_z)),
        mesh=mesh,
        in_specs=(
            P(None, None, ("aux", "ao"), None),
            P("ao", None),
            P("ao", None),
            P(),
            P("ao", None),
            P("ao"),
        ),
        out_specs=P(None, ("aux", "ao"), None),
        check_vma=False,
    )
```

```python
import functools

import jax
import jax.numpy as jnp
from jax import lax
from jax.experimental import pallas as pl
from jax.experimental.pallas import tpu as pltpu
from jax.sharding import PartitionSpec as P

MESH = pl.DeviceIdType.MESH
F32 = jnp.float32
BF16 = jnp.bfloat16
NB = 32
TILE = NB * NB
QUART = 256
HALF = 128
SLOTS = 8
CORES = 2


def iota(shape, dim):
    return lax.broadcasted_iota(jnp.int32, shape, dim)


def dot(a, b):
    return lax.dot_general(a, b, (((1,), (0,)), ((), ())), preferred_element_type=F32)


def dot_nt(a, b):
    return lax.dot_general(a, b, (((1,), (1,)), ((), ())), preferred_element_type=F32)


def ones_where(cond):
    return jnp.where(cond, 1.0, 0.0).astype(BF16)


def pick(rows, cond):
    return jnp.sum(jnp.where(cond, rows, 0.0), axis=0, keepdims=True)


def lane_sum(values):
    return jnp.sum(values, axis=1, keepdims=True)


def wait_bytes(ref, sem):
    pltpu.make_async_copy(ref, ref, sem).wait()


def kernel(
    dims, b_hbm, pairs_own, live_own, occ_own, virt_own, sizes, out_ref, flag_ref,
    b_in, bq, meta, table, send, recv, zup, masked, masked_up, w1, w2, v1, v2,
    same, cross, rs, rs_in,
    b_sem, meta_sem, table_sem, small_send, send_sem, recv_sem, zs_sem, zu_sem, rs_sem,
):
    caps, n_x, n_y, n_z = dims
    span = max(caps)
    n_grp = n_y * CORES
    n_ao = n_x * n_grp
    n_p = 2 * n_ao
    n_c = n_ao * SLOTS * 2
    me = lax.axis_index("ao")
    zz = lax.axis_index("aux")
    above = lax.rem(zz + 1, n_z)
    below = lax.rem(zz + n_z - 1, n_z)
    my_x = me // n_grp
    my_in = lax.rem(me, n_grp)
    my_y = my_in // CORES
    my_core = lax.rem(me, CORES)

    def device(x, y, core):
        return (x * n_y + y) * CORES + core

    def by_core(core, act):
        if caps[0] == caps[1]:
            act(0, caps[0])
            return
        for c in range(CORES):
            pl.when(core == c)(functools.partial(act, c, caps[c]))

    load_b = pltpu.make_async_copy(b_hbm, b_in, b_sem)
    load_b.start()
    if min(caps) < span:
        unused = slice(min(caps) * HALF, span * HALF)
        for buffer in (recv, zup):
            buffer[:, :, unused] = jnp.zeros((n_ao, 16, (span - min(caps)) * HALF), BF16)

    spot = (my_core * n_x + my_x) * n_y + my_y
    line = (my_core * n_x + my_x) * n_y
    lane = iota((1, 128), 1)
    facts = jnp.where(lane == SLOTS, live_own[...].astype(F32), jnp.zeros((1, 128), F32))
    pairs = pairs_own[...].astype(F32)
    for k in range(SLOTS):
        facts = jnp.where(lane == k, pairs[:, k:k + 1], facts)
    meta[pl.ds(spot, 1)] = facts.reshape(1, 1, 128)
    greens = [own[:, i * 128:(i + 1) * 128].astype(F32) for own in (occ_own[...], virt_own[...]) for i in range(8)]
    table[pl.ds(spot, 1)] = jnp.concatenate(greens, axis=0).astype(BF16).reshape(1, 16, 128)

    barrier = pltpu.get_barrier_semaphore()

    def greet(step, carry):
        peer = lax.rem(me + step, n_ao)
        pl.semaphore_signal(barrier, inc=1, device_id=(zz, peer), device_id_type=MESH)
        return carry

    pl.semaphore_signal(barrier, inc=1, device_id=(below, me), device_id_type=MESH)
    lax.fori_loop(1, n_ao, greet, 0, unroll=7)

    lane_in, lane_out = iota((512, 512), 0), iota((512, 512), 1)
    moved = (lane_in // 16 % 2) * 256 + (lane_in // 32) * 16 + lane_in % 16
    mover = ones_where(moved == lane_out)
    part_atoms = n_ao // 4
    part_rows = part_atoms * SLOTS * 2

    def reorder(part, carry):
        loaded = b_in[pl.ds(part * part_atoms, part_atoms)].reshape(part_rows, TILE)
        rows = pl.ds(pl.multiple_of(part * part_rows, part_rows), part_rows)
        for mh in range(2):
            placed = dot(loaded[:, mh * 512:(mh + 1) * 512], mover).astype(BF16)
            bq[2 * mh, rows, :] = placed[:, :QUART]
            bq[2 * mh + 1, rows, :] = placed[:, QUART:]
        return carry

    pl.semaphore_wait(barrier, n_ao)

    def spread_y(ref, send_to, recv_from):
        def one(step, carry):
            peer = device(my_x, lax.rem(my_y + step, n_y), my_core)
            pltpu.make_async_remote_copy(
                src_ref=ref.at[spot], dst_ref=ref.at[spot], send_sem=send_to, recv_sem=recv_from,
                device_id=(zz, peer), device_id_type=MESH,
            ).start()
            return carry

        lax.fori_loop(1, n_y, one, 0)

    n_a = n_x * CORES
    mine = my_x * CORES + my_core

    def spread_x(ref, send_to, recv_from):
        block = pl.ds(line, n_y)

        def one(step, carry):
            to = lax.rem(mine + step, n_a)
            pltpu.make_async_remote_copy(
                src_ref=ref.at[block], dst_ref=ref.at[block], send_sem=send_to, recv_sem=recv_from,
                device_id=(zz, device(to // CORES, my_y, lax.rem(to, CORES))), device_id_type=MESH,
            ).start()
            return carry

        lax.fori_loop(1, n_a, one, 0)

    n_far = (n_a - 1) * n_y

    def tell(step, carry):
        peer = lax.rem(me + step, n_ao)
        pltpu.make_async_remote_copy(
            src_ref=meta.at[spot], dst_ref=meta.at[spot], send_sem=small_send.at[0], recv_sem=meta_sem,
            device_id=(zz, peer), device_id_type=MESH,
        ).start()
        return carry

    lax.fori_loop(1, n_ao, tell, 0, unroll=7)
    spread_y(table, small_send.at[1], table_sem.at[0])
    load_b.wait()
    lax.fori_loop(0, 4, reorder, 0)

    c_row = iota((1, n_c), 1)
    c_atom, c_slot, c_aux = c_row // 16, c_row // 2 % 8, c_row % 2
    earlier = ones_where((iota((128, 128), 0) // 2 < iota((128, 128), 1) // 2) & (iota((128, 128), 0) % 2 == 0))
    atom_col = iota((n_ao, n_c), 0)
    spot_col = device(atom_col // n_y % n_x, atom_col % n_y, atom_col // (n_x * n_y))
    own_col = spot_col == iota((n_ao, n_c), 1) // 16
    slot_pick = ones_where(iota((128, n_c), 0) == iota((128, n_c), 1) // 2 % 8)
    size_row = jnp.broadcast_to(sizes[...].astype(F32), (n_ao, n_ao))
    size_col = lane_sum(jnp.where(iota((n_ao, n_ao), 0) == iota((n_ao, n_ao), 1), size_row, 0.0))
    size_all = jnp.broadcast_to(size_col, (n_ao, n_c))
    row_big = pick(size_all, atom_col == iota((n_ao, n_c), 1) // 16) > 16.5

    wait_bytes(table.at[pl.ds(0, n_y - 1)], table_sem.at[0])
    spread_x(table, small_send.at[2], table_sem.at[1])
    wait_bytes(meta.at[pl.ds(0, n_ao - 1)], meta_sem)
    facts = meta[...].reshape(n_ao, 128)
    c_col = pick(dot(facts.astype(BF16), slot_pick), own_col)
    c_live = pick(jnp.broadcast_to(facts[:, SLOTS:SLOTS + 1], (n_ao, n_c)), own_col)
    col_big = pick(size_all, atom_col.astype(F32) == c_col) > 16.5
    alive = c_slot.astype(F32) < c_live
    one = jnp.ones((1, n_c), F32)
    nil = jnp.zeros((1, n_c), F32)
    big = jnp.where(row_big, one, nil)
    wide = jnp.where(col_big, one, nil)
    here = jnp.where(alive, one, nil)
    is4 = here * big * wide
    is2r = here * big * (one - wide)
    is2c = here * (one - big) * wide
    is1 = here * (one - big) * (one - wide)
    marks = jnp.concatenate([is4, is2c, is2r, is1, jnp.zeros((12, n_c), F32)], axis=0)
    marks = [marks[:, i * 128:(i + 1) * 128] for i in range(n_c // 128)]
    inside = dot(jnp.concatenate(marks, axis=0).astype(BF16), earlier)
    before, count = [], jnp.zeros((16, 1), F32)
    for i, block in enumerate(marks):
        before.append(inside[i * 16:(i + 1) * 16] + count)
        count = count + lane_sum(block) * 0.5
    before = jnp.concatenate(before, axis=1)
    base2c = 4.0 * count[0:1]
    base2r = base2c + 4.0 * jnp.floor((count[1:2] + 1.0) * 0.5)
    base1 = base2r + 2.0 * count[2:3]
    total = base1 + count[3:4]
    twos = jnp.floor(before[1:2] * 0.5)
    first = is4 * 4.0 * before[0:1] + is2c * (base2c + before[1:2] + 2.0 * twos)
    first = first + is2r * (base2r + 2.0 * before[2:3]) + is1 * (base1 + before[3:4])
    c_auxf = c_aux.astype(F32)

    def numbered(member, offset):
        return jnp.where(member > 0.5, 2.0 * (first + offset) + c_auxf, -5.0)

    units = [
        numbered(here, 0.0),
        numbered(is4 + is2c, 2.0),
        numbered(is4 + is2r, 1.0),
        numbered(is4, 3.0),
    ]
    flag_ref[...] = jnp.where(total > 4.0 * sum(caps) * (n_ao // CORES), 1, 0)

    unit_lanes = jnp.concatenate(units, axis=1)
    n_half = n_y // 2
    my_odd = lax.rem(my_y, 2)
    turns = 2 * n_x

    def place(x, y, core):
        return ((x * 2 + lax.rem(y, 2)) * n_half + y // 2) * CORES + core

    my_place = place(my_x, my_y, my_core)

    def offset(even, k):
        odd_off, even_off = (1, -1, 3, -3)[k], (2, -2, 4, 0)[k]
        return odd_off + even * (even_off - odd_off)

    out_row = iota((span * n_y * 8, 1), 0)
    out_lo, out_slot = out_row // 8 % n_y, out_row // (8 * n_y)
    out_core = out_lo % CORES
    out_first = (out_lo // CORES) * sum(caps) + out_core * caps[0] + out_slot
    out_unit = out_first * 8 + (out_row % 4) * 2 + out_row // 4 % 2
    out_keep = out_slot < jnp.where(out_core == 0, caps[0], caps[1])

    def pack(turn):
        to_x = lax.rem(my_x + turn // 2, n_x)
        even = lax.rem(turn, 2)
        grp = to_x * 2 + lax.rem(my_odd + 1 + even, 2)
        wanted = jnp.where(out_keep, out_unit + grp * (n_y // CORES * sum(caps) * 8), -99).astype(F32)
        got = dot(ones_where(unit_lanes == wanted), bq[...].reshape(4 * n_c, QUART))
        for j in range(span):
            part = got[j * n_y * 8:(j + 1) * n_y * 8]
            both = [part[:, h * HALF:(h + 1) * HALF].reshape(n_y, 8, HALF) for h in range(2)]
            send[pl.ds(grp * n_y, n_y), :, j * HALF:(j + 1) * HALF] = jnp.concatenate(both, axis=1).astype(BF16)

        for k in range(n_half):
            to_y = lax.rem(my_y + n_y + offset(even, k), n_y)
            for flip in range(CORES):
                core = lax.rem(my_core + flip, CORES)
                peer = device(to_x, to_y, core)
                at = place(to_x, to_y, core)

                def act(c, count):
                    source = send.at[at, :, pl.ds(0, count * HALF)]
                    target = recv.at[my_place, :, pl.ds(0, count * HALF)]

                    @pl.when(peer != me)
                    def _():
                        pltpu.make_async_remote_copy(
                            src_ref=source, dst_ref=target, send_sem=send_sem.at[c], recv_sem=recv_sem.at[turn * n_half + k],
                            device_id=(zz, peer), device_id_type=MESH,
                        ).start()

                    @pl.when(peer == me)
                    def _():
                        pltpu.make_async_copy(source, target, recv_sem.at[turn * n_half + k]).start()

                by_core(core, act)

    def origin(turn):
        return lax.rem(my_x + n_x - turn // 2, n_x) * 2 + lax.rem(my_odd + 1 + turn, 2)

    def forward(turn):
        from_x = lax.rem(my_x + n_x - turn // 2, n_x)
        for k in range(n_half):
            from_y = lax.rem(my_y + n_y - offset(lax.rem(turn, 2), k), n_y)
            chip = place(from_x, from_y, 0)

            def act(c, count):
                block = (pl.ds(chip, CORES), slice(None), pl.ds(0, count * HALF))
                wait_bytes(recv.at[block], recv_sem.at[turn * n_half + k])
                pltpu.make_async_remote_copy(
                    src_ref=recv.at[block], dst_ref=zup.at[block], send_sem=zs_sem, recv_sem=zu_sem.at[turn],
                    device_id=(above, me), device_id_type=MESH,
                ).start()

            by_core(my_core, act)

    lag = 3

    def pack_and_forward(turn, carry):
        pack(turn)
        pl.when(turn >= lag)(lambda: forward(turn - lag))
        return carry

    lax.fori_loop(0, turns, pack_and_forward, 0)

    pair = iota((span * 16, 1), 0)
    slot_base = ((my_place // CORES) * sum(caps) + my_core * caps[0] + pair // 16) * 4
    lead = ((slot_base + pair // 4 % 4) * 2).astype(F32)
    tail = ((slot_base + pair % 4) * 2).astype(F32)
    c_tile = (c_row // 2).astype(F32)

    def describe(unit):
        tile, atom, col, quarter, valid = (jnp.zeros((span * 16, 1), F32) for _ in range(5))
        for q in range(4):
            hit = units[q] == unit
            tile = tile + lane_sum(jnp.where(hit, c_tile, 0.0))
            atom = atom + lane_sum(jnp.where(hit, c_atom.astype(F32), 0.0))
            col = col + lane_sum(jnp.where(hit, c_col, 0.0))
            count = lane_sum(jnp.where(hit, 1.0, 0.0))
            quarter = quarter + q * count
            valid = valid + count
        row_half = jnp.where(quarter > 1.5, 1.0, 0.0)
        return tile, atom, col, row_half, quarter - 2.0 * row_half, valid

    tile_a, atom_a, col_a, mh_a, nh_a, valid_a = describe(lead)
    tile_b, _, _, mh_b, nh_b, valid_b = describe(tail)
    joined = (tile_a == tile_b) & (valid_a > 0.5) & (valid_b > 0.5)
    index1 = jnp.where(joined & (nh_a == nh_b), atom_a * 16.0 + 4.0 * mh_b, -99.0)
    index2 = jnp.where(joined & (mh_a == mh_b), col_a * 16.0 + 8.0 + 4.0 * nh_a, -99.0)
    wait_bytes(table.at[pl.ds(0, n_far)], table_sem.at[1])
    greens = table[...].reshape(n_ao * 16, 128)
    g_row = iota((span * 16, n_ao * 16), 1)
    g_spot = g_row // 16
    g_atom = device(g_spot // n_y % n_x, g_spot % n_y, g_spot // (n_x * n_y))
    g_lane = (g_atom * 16 + g_row % 16).astype(F32)
    for target, index, half in ((v1, index1, mh_a), (v2, index2, nh_b)):
        rows = [dot(ones_where(g_lane == index + i), greens).astype(BF16) for i in range(4)]
        rows = dot(jnp.concatenate(rows, axis=1), mover)
        target[...] = jnp.where(half < 0.5, rows[:, :QUART], rows[:, QUART:])

    r, s = iota((QUART, QUART), 0), iota((QUART, QUART), 1)
    hi, lo = r // 16, r % 16
    spread1, gather1, keep1 = ones_where(hi == s % 16), ones_where(hi == s // 16), ones_where(lo == s % 16)
    spread2, gather2, keep2 = ones_where(lo == s // 16), ones_where(lo == s % 16), ones_where(hi == s // 16)

    def weights(j):
        for m in range(2):
            for a in range(2):
                for b in range(2):
                    rows, lanes = slice(a * QUART, (a + 1) * QUART), slice(b * QUART, (b + 1) * QUART)
                    vec = v1[pl.ds(j * 16 + (2 * m + a) * 4 + 2 * m + b, 1), :].astype(BF16)
                    w1[j, m, rows, lanes] = dot(spread1 * vec, gather1).astype(BF16) * keep1
                    vec = v2[pl.ds(j * 16 + (2 * a + m) * 4 + 2 * b + m, 1), :].astype(BF16)
                    w2[j, m, rows, lanes] = dot(spread2 * vec, gather2).astype(BF16) * keep2

    o, i = iota((n_y * 16, n_y * 16), 0), iota((n_y * 16, n_y * 16), 1)
    went = (i // 8 % 2 * 4 + i % 4) * (2 * n_y) + (i // 16) * 2 + i // 4 % 2
    sorter = ones_where(o == went)

    def unpack(source, turn, target):
        grp = origin(turn)
        block = source[pl.ds(grp * n_y, n_y)].reshape(n_y * 16, span * HALF)
        placed = dot(sorter, block).astype(BF16)
        rows = pl.ds(pl.multiple_of(grp * (2 * n_y), 2 * n_y), 2 * n_y)
        for h in range(2):
            for b in range(4):
                part = placed[(h * 4 + b) * 2 * n_y:(h * 4 + b + 1) * 2 * n_y]
                for j in range(span):
                    target[j, rows, b * QUART + h * HALF:b * QUART + (h + 1) * HALF] = part[:, j * HALF:(j + 1) * HALF]

    def contract(tiles, j):
        half = [dot(tiles[:, m * 512:(m + 1) * 512], w1[j, m]).astype(BF16) for m in range(2)]
        done = []
        for m in range(2):
            lanes = slice(m * QUART, (m + 1) * QUART)
            done.append(dot(jnp.concatenate([part[:, lanes] for part in half], axis=1), w2[j, m]).astype(BF16))
        return jnp.concatenate([done[m][:, a * QUART:(a + 1) * QUART] for a in range(2) for m in range(2)], axis=1)

    def weights_and_forward(j, carry):
        weights(j)
        for turn in range(turns - lag, turns):
            pl.when(j == (turn - turns + lag) * span // lag)(functools.partial(forward, turn))
        return carry

    lax.fori_loop(0, span, weights_and_forward, 0)

    def arrive(turn, carry):
        unpack(recv, turn, masked)
        return carry

    lax.fori_loop(0, turns, arrive, 0)

    same[...] = jnp.zeros_like(same)

    q, p = iota((n_p, n_p), 0), iota((n_p, n_p), 1)
    straight = ones_where(place(q // (4 * n_y), q // 4 % n_y, q // 2 % 2) * 2 + q % 2 == p)

    def own_slot(j, carry):
        tiles = masked[j]
        ordered = dot(straight, tiles).astype(BF16)
        same[...] += dot_nt(contract(tiles, j), ordered)
        masked[j] = ordered
        return carry

    lax.fori_loop(0, span, own_slot, 0)

    def scatter(c, part):
        for e in range(2):
            rs[c, :, e, :] = part[pl.ds(e, n_ao, stride=2), :]
        rs_in[c, pl.ds(my_place, 1)] = rs[c, pl.ds(my_place, 1)]

        def one(step, carry):
            peer = lax.rem(me + step, n_ao)
            at = place(peer // n_grp, peer // CORES % n_y, peer % CORES)
            pltpu.make_async_remote_copy(
                src_ref=rs.at[c, at], dst_ref=rs_in.at[c, my_place], send_sem=rs_sem.at[c], recv_sem=rs_sem.at[2 + c],
                device_id=(zz, peer), device_id_type=MESH,
            ).start()
            return carry

        lax.fori_loop(1, n_ao, one, 0, unroll=7)

    def gather(c):
        wait_bytes(rs_in.at[c, pl.ds(0, n_ao - 1)], rs_sem.at[2 + c])
        out_ref[c] = jnp.sum(rs_in[c], axis=0)

    scatter(0, same)

    def arrive_up(turn, carry):
        def act(c, count):
            wait_bytes(zup.at[pl.ds(origin(turn) * n_y, n_y), :, pl.ds(0, count * HALF)], zu_sem.at[turn])

        by_core(my_core, act)
        unpack(zup, turn, masked_up)
        return carry

    lax.fori_loop(0, turns, arrive_up, 0)
    cross[...] = jnp.zeros_like(cross)

    def up_slot(j, carry):
        cross[...] += dot_nt(contract(masked_up[j], j), masked[j])
        return carry

    lax.fori_loop(0, span, up_slot, 0)
    scatter(1, cross)
    gather(0)
    gather(1)

    wait_bytes(meta.at[pl.ds(0, n_ao - 1)], small_send.at[0])
    wait_bytes(table.at[pl.ds(0, n_y - 1)], small_send.at[1])
    wait_bytes(table.at[pl.ds(0, n_far)], small_send.at[2])
    if caps[0] == caps[1]:
        wait_bytes(send.at[pl.ds(0, n_ao - 1)], send_sem.at[0])
    else:
        for c in range(CORES):
            lanes = pl.ds(0, caps[c] * HALF)

            @pl.when(my_core == c)
            def _():
                wait_bytes(send.at[pl.ds(0, n_ao // CORES - 1), :, lanes], send_sem.at[c])

            @pl.when(my_core != c)
            def _():
                wait_bytes(send.at[pl.ds(0, n_ao // CORES), :, lanes], send_sem.at[c])

    def sent_up(c, count):
        wait_bytes(zup.at[:, :, pl.ds(0, count * HALF)], zs_sem)

    by_core(my_core, sent_up)
    for c in range(2):
        wait_bytes(rs.at[c, pl.ds(0, n_ao - 1)], rs_sem.at[c])


def run(caps, shape, ident, b_source, pair_cols, live_slots, g_occ, g_virt, atom_sizes):
    n_x, n_y, n_z = shape
    n_ao = n_x * n_y * CORES
    n_c, n_p = n_ao * SLOTS * 2, 2 * n_ao
    span = max(caps)
    vmem = pl.BlockSpec(memory_space=pltpu.VMEM)
    dma = pltpu.SemaphoreType.DMA
    return pl.pallas_call(
        functools.partial(kernel, (caps, n_x, n_y, n_z)),
        out_shape=(jax.ShapeDtypeStruct((2, 2, n_p), F32), jax.ShapeDtypeStruct((1, 1), jnp.int32)),
        in_specs=[pl.BlockSpec(memory_space=pl.ANY)] + [vmem] * 5,
        out_specs=(vmem, vmem),
        scratch_shapes=[
            pltpu.VMEM((n_ao, SLOTS, 2, TILE), BF16),
            pltpu.VMEM((4, n_c, QUART), BF16),
            pltpu.VMEM((n_ao, 1, 128), F32),
            pltpu.VMEM((n_ao, 16, 128), BF16),
            pltpu.VMEM((n_ao, 16, span * HALF), BF16),
            pltpu.VMEM((n_ao, 16, span * HALF), BF16),
            pltpu.VMEM((n_ao, 16, span * HALF), BF16),
            pltpu.VMEM((span, n_p, TILE), BF16),
            pltpu.VMEM((span, n_p, TILE), BF16),
            pltpu.VMEM((span, 2, 512, 512), BF16),
            pltpu.VMEM((span, 2, 512, 512), BF16),
            pltpu.VMEM((span * 16, QUART), F32),
            pltpu.VMEM((span * 16, QUART), F32),
            pltpu.VMEM((n_p, n_p), F32),
            pltpu.VMEM((n_p, n_p), F32),
            pltpu.VMEM((2, n_ao, 2, n_p), F32),
            pltpu.VMEM((2, n_ao, 2, n_p), F32),
            dma, dma, dma((2,)), dma((3,)), dma((2,)), dma((n_x * n_y,)), dma, dma((2 * n_x,)), dma((4,)),
        ],
        compiler_params=pltpu.CompilerParams(
            collective_id=ident, has_side_effects=True, vmem_limit_bytes=56 * 1024 * 1024
        ),
        name=f"blocks_{sum(caps)}",
    )(b_source, pair_cols, live_slots, g_occ, g_virt, atom_sizes)


def whole(shape, values):
    return run((8, 8), shape, 1, *values)[0]


def local(shape, b_source, g_occ, g_virt, atom_sizes, pair_cols, live_slots):
    given = (b_source, pair_cols, live_slots.reshape(1, 1), g_occ, g_virt, atom_sizes.reshape(1, -1))
    short, flag = run((4, 3), shape, 0, *given)
    return lax.cond(
        flag[0, 0] > 0, lambda *values: whole(shape, values), lambda *values: short, *given
    )


def solution(mesh):
    n_ao, n_z = mesh.shape["ao"], mesh.shape["aux"]
    n_x = 4 if n_ao >= 64 else 2
    return jax.shard_map(
        functools.partial(local, (n_x, n_ao // (n_x * CORES), n_z)),
        mesh=mesh,
        in_specs=(
            P(None, None, ("aux", "ao"), None),
            P("ao", None),
            P("ao", None),
            P(),
            P("ao", None),
            P("ao"),
        ),
        out_specs=P(None, ("aux", "ao"), None),
        check_vma=False,
    )
```

```python
import functools

import jax
import jax.numpy as jnp
from jax import lax
from jax.experimental import pallas as pl
from jax.experimental.pallas import tpu as pltpu
from jax.sharding import PartitionSpec as P

MESH = pl.DeviceIdType.MESH
F32 = jnp.float32
BF16 = jnp.bfloat16
NB = 32
TILE = NB * NB
QUART = 256
HALF = 128
SLOTS = 8
CORES = 2


def iota(shape, dim):
    return lax.broadcasted_iota(jnp.int32, shape, dim)


def dot(a, b):
    return lax.dot_general(a, b, (((1,), (0,)), ((), ())), preferred_element_type=F32)


def dot_nt(a, b):
    return lax.dot_general(a, b, (((1,), (1,)), ((), ())), preferred_element_type=F32)


def ones_where(cond):
    return jnp.where(cond, 1.0, 0.0).astype(BF16)


def pick(rows, cond):
    return jnp.sum(jnp.where(cond, rows, 0.0), axis=0, keepdims=True)


def lane_sum(values):
    return jnp.sum(values, axis=1, keepdims=True)


def wait_bytes(ref, sem):
    pltpu.make_async_copy(ref, ref, sem).wait()


def kernel(
    dims, b_hbm, pairs_own, live_own, occ_own, virt_own, sizes, out_ref, flag_ref,
    b_in, bq, meta, table, send, recv, zup, masked, masked_up, w1, w2, v1, v2,
    same, cross, rs, rs_in,
    b_sem, meta_sem, table_sem, small_send, send_sem, recv_sem, zs_sem, zu_sem, rs_sem,
):
    caps, n_x, n_y, n_z = dims
    span = max(caps)
    n_grp = n_y * CORES
    n_ao = n_x * n_grp
    n_p = 2 * n_ao
    n_c = n_ao * SLOTS * 2
    me = lax.axis_index("ao")
    zz = lax.axis_index("aux")
    above = lax.rem(zz + 1, n_z)
    below = lax.rem(zz + n_z - 1, n_z)
    my_x = me // n_grp
    my_in = lax.rem(me, n_grp)
    my_y = my_in // CORES
    my_core = lax.rem(me, CORES)

    def device(x, y, core):
        return (x * n_y + y) * CORES + core

    def by_core(core, act):
        if caps[0] == caps[1]:
            act(0, caps[0])
            return
        for c in range(CORES):
            pl.when(core == c)(functools.partial(act, c, caps[c]))

    load_b = pltpu.make_async_copy(b_hbm, b_in, b_sem)
    load_b.start()
    if min(caps) < span:
        unused = slice(min(caps) * HALF, span * HALF)
        for buffer in (recv, zup):
            buffer[:, :, unused] = jnp.zeros((n_ao, 16, (span - min(caps)) * HALF), BF16)

    spot = (my_core * n_x + my_x) * n_y + my_y
    line = (my_core * n_x + my_x) * n_y
    lane = iota((1, 128), 1)
    facts = jnp.where(lane == SLOTS, live_own[...].astype(F32), jnp.zeros((1, 128), F32))
    pairs = pairs_own[...].astype(F32)
    for k in range(SLOTS):
        facts = jnp.where(lane == k, pairs[:, k:k + 1], facts)
    meta[pl.ds(spot, 1)] = facts.reshape(1, 1, 128)
    greens = [own[:, i * 128:(i + 1) * 128].astype(F32) for own in (occ_own[...], virt_own[...]) for i in range(8)]
    table[pl.ds(spot, 1)] = jnp.concatenate(greens, axis=0).astype(BF16).reshape(1, 16, 128)

    barrier = pltpu.get_barrier_semaphore()

    def greet(step, carry):
        peer = lax.rem(me + step, n_ao)
        pl.semaphore_signal(barrier, inc=1, device_id=(zz, peer), device_id_type=MESH)
        return carry

    pl.semaphore_signal(barrier, inc=1, device_id=(below, me), device_id_type=MESH)
    lax.fori_loop(1, n_ao, greet, 0, unroll=7)

    lane_in, lane_out = iota((512, 512), 0), iota((512, 512), 1)
    moved = (lane_in // 16 % 2) * 256 + (lane_in // 32) * 16 + lane_in % 16
    mover = ones_where(moved == lane_out)
    part_atoms = n_ao // 4
    part_rows = part_atoms * SLOTS * 2

    def reorder(part, carry):
        loaded = b_in[pl.ds(part * part_atoms, part_atoms)].reshape(part_rows, TILE)
        rows = pl.ds(pl.multiple_of(part * part_rows, part_rows), part_rows)
        for mh in range(2):
            placed = dot(loaded[:, mh * 512:(mh + 1) * 512], mover).astype(BF16)
            bq[2 * mh, rows, :] = placed[:, :QUART]
            bq[2 * mh + 1, rows, :] = placed[:, QUART:]
        return carry

    load_b.wait()
    lax.fori_loop(0, 3, reorder, 0)
    pl.semaphore_wait(barrier, n_ao)

    def spread_y(ref, send_to, recv_from):
        def one(step, carry):
            peer = device(my_x, lax.rem(my_y + step, n_y), my_core)
            pltpu.make_async_remote_copy(
                src_ref=ref.at[spot], dst_ref=ref.at[spot], send_sem=send_to, recv_sem=recv_from,
                device_id=(zz, peer), device_id_type=MESH,
            ).start()
            return carry

        lax.fori_loop(1, n_y, one, 0)

    n_a = n_x * CORES
    mine = my_x * CORES + my_core

    def spread_x(ref, send_to, recv_from):
        block = pl.ds(line, n_y)

        def one(step, carry):
            to = lax.rem(mine + step, n_a)
            pltpu.make_async_remote_copy(
                src_ref=ref.at[block], dst_ref=ref.at[block], send_sem=send_to, recv_sem=recv_from,
                device_id=(zz, device(to // CORES, my_y, lax.rem(to, CORES))), device_id_type=MESH,
            ).start()
            return carry

        lax.fori_loop(1, n_a, one, 0)

    n_far = (n_a - 1) * n_y

    def tell(step, carry):
        peer = lax.rem(me + step, n_ao)
        pltpu.make_async_remote_copy(
            src_ref=meta.at[spot], dst_ref=meta.at[spot], send_sem=small_send.at[0], recv_sem=meta_sem,
            device_id=(zz, peer), device_id_type=MESH,
        ).start()
        return carry

    lax.fori_loop(1, n_ao, tell, 0, unroll=7)
    lax.fori_loop(3, 4, reorder, 0)
    spread_y(table, small_send.at[1], table_sem.at[0])

    c_row = iota((1, n_c), 1)
    c_atom, c_slot, c_aux = c_row // 16, c_row // 2 % 8, c_row % 2
    earlier = ones_where((iota((128, 128), 0) // 2 < iota((128, 128), 1) // 2) & (iota((128, 128), 0) % 2 == 0))
    atom_col = iota((n_ao, n_c), 0)
    spot_col = device(atom_col // n_y % n_x, atom_col % n_y, atom_col // (n_x * n_y))
    own_col = spot_col == iota((n_ao, n_c), 1) // 16
    slot_pick = ones_where(iota((128, n_c), 0) == iota((128, n_c), 1) // 2 % 8)
    size_row = jnp.broadcast_to(sizes[...].astype(F32), (n_ao, n_ao))
    size_col = lane_sum(jnp.where(iota((n_ao, n_ao), 0) == iota((n_ao, n_ao), 1), size_row, 0.0))
    size_all = jnp.broadcast_to(size_col, (n_ao, n_c))
    row_big = pick(size_all, atom_col == iota((n_ao, n_c), 1) // 16) > 16.5

    wait_bytes(table.at[pl.ds(0, n_y - 1)], table_sem.at[0])
    spread_x(table, small_send.at[2], table_sem.at[1])
    wait_bytes(meta.at[pl.ds(0, n_ao - 1)], meta_sem)
    facts = meta[...].reshape(n_ao, 128)
    c_col = pick(dot(facts.astype(BF16), slot_pick), own_col)
    c_live = pick(jnp.broadcast_to(facts[:, SLOTS:SLOTS + 1], (n_ao, n_c)), own_col)
    col_big = pick(size_all, atom_col.astype(F32) == c_col) > 16.5
    alive = c_slot.astype(F32) < c_live
    one = jnp.ones((1, n_c), F32)
    nil = jnp.zeros((1, n_c), F32)
    big = jnp.where(row_big, one, nil)
    wide = jnp.where(col_big, one, nil)
    here = jnp.where(alive, one, nil)
    is4 = here * big * wide
    is2r = here * big * (one - wide)
    is2c = here * (one - big) * wide
    is1 = here * (one - big) * (one - wide)
    marks = jnp.concatenate([is4, is2c, is2r, is1, jnp.zeros((12, n_c), F32)], axis=0)
    marks = [marks[:, i * 128:(i + 1) * 128] for i in range(n_c // 128)]
    inside = dot(jnp.concatenate(marks, axis=0).astype(BF16), earlier)
    before, count = [], jnp.zeros((16, 1), F32)
    for i, block in enumerate(marks):
        before.append(inside[i * 16:(i + 1) * 16] + count)
        count = count + lane_sum(block) * 0.5
    before = jnp.concatenate(before, axis=1)
    base2c = 4.0 * count[0:1]
    base2r = base2c + 4.0 * jnp.floor((count[1:2] + 1.0) * 0.5)
    base1 = base2r + 2.0 * count[2:3]
    total = base1 + count[3:4]
    twos = jnp.floor(before[1:2] * 0.5)
    first = is4 * 4.0 * before[0:1] + is2c * (base2c + before[1:2] + 2.0 * twos)
    first = first + is2r * (base2r + 2.0 * before[2:3]) + is1 * (base1 + before[3:4])
    c_auxf = c_aux.astype(F32)

    def numbered(member, offset):
        return jnp.where(member > 0.5, 2.0 * (first + offset) + c_auxf, -5.0)

    units = [
        numbered(here, 0.0),
        numbered(is4 + is2c, 2.0),
        numbered(is4 + is2r, 1.0),
        numbered(is4, 3.0),
    ]
    flag_ref[...] = jnp.where(total > 4.0 * sum(caps) * (n_ao // CORES), 1, 0)

    unit_lanes = jnp.concatenate(units, axis=1)
    n_half = n_y // 2
    my_odd = lax.rem(my_y, 2)
    turns = 2 * n_x

    def place(x, y, core):
        return ((x * 2 + lax.rem(y, 2)) * n_half + y // 2) * CORES + core

    my_place = place(my_x, my_y, my_core)

    def offset(even, k):
        odd_off, even_off = (1, -1, 3, -3)[k], (2, -2, 4, 0)[k]
        return odd_off + even * (even_off - odd_off)

    out_row = iota((span * n_y * 8, 1), 0)
    out_lo, out_slot = out_row // 8 % n_y, out_row // (8 * n_y)
    out_core = out_lo % CORES
    out_first = (out_lo // CORES) * sum(caps) + out_core * caps[0] + out_slot
    out_unit = out_first * 8 + (out_row % 4) * 2 + out_row // 4 % 2
    out_keep = out_slot < jnp.where(out_core == 0, caps[0], caps[1])

    def pack(turn):
        to_x = lax.rem(my_x + turn // 2, n_x)
        even = lax.rem(turn, 2)
        grp = to_x * 2 + lax.rem(my_odd + 1 + even, 2)
        wanted = jnp.where(out_keep, out_unit + grp * (n_y // CORES * sum(caps) * 8), -99).astype(F32)
        got = dot(ones_where(unit_lanes == wanted), bq[...].reshape(4 * n_c, QUART))
        for j in range(span):
            part = got[j * n_y * 8:(j + 1) * n_y * 8]
            both = [part[:, h * HALF:(h + 1) * HALF].reshape(n_y, 8, HALF) for h in range(2)]
            send[pl.ds(grp * n_y, n_y), :, j * HALF:(j + 1) * HALF] = jnp.concatenate(both, axis=1).astype(BF16)

        for k in range(n_half):
            to_y = lax.rem(my_y + n_y + offset(even, k), n_y)
            for flip in range(CORES):
                core = lax.rem(my_core + flip, CORES)
                peer = device(to_x, to_y, core)
                at = place(to_x, to_y, core)

                def act(c, count):
                    source = send.at[at, :, pl.ds(0, count * HALF)]
                    target = recv.at[my_place, :, pl.ds(0, count * HALF)]

                    @pl.when(peer != me)
                    def _():
                        pltpu.make_async_remote_copy(
                            src_ref=source, dst_ref=target, send_sem=send_sem.at[c], recv_sem=recv_sem.at[turn * n_half + k],
                            device_id=(zz, peer), device_id_type=MESH,
                        ).start()

                    @pl.when(peer == me)
                    def _():
                        pltpu.make_async_copy(source, target, recv_sem.at[turn * n_half + k]).start()

                by_core(core, act)

    def origin(turn):
        return lax.rem(my_x + n_x - turn // 2, n_x) * 2 + lax.rem(my_odd + 1 + turn, 2)

    def forward(turn):
        from_x = lax.rem(my_x + n_x - turn // 2, n_x)
        for k in range(n_half):
            from_y = lax.rem(my_y + n_y - offset(lax.rem(turn, 2), k), n_y)
            chip = place(from_x, from_y, 0)

            def act(c, count):
                block = (pl.ds(chip, CORES), slice(None), pl.ds(0, count * HALF))
                wait_bytes(recv.at[block], recv_sem.at[turn * n_half + k])
                pltpu.make_async_remote_copy(
                    src_ref=recv.at[block], dst_ref=zup.at[block], send_sem=zs_sem, recv_sem=zu_sem.at[turn],
                    device_id=(above, me), device_id_type=MESH,
                ).start()

            by_core(my_core, act)

    lag = 3

    def pack_and_forward(turn, carry):
        pack(turn)
        pl.when(turn >= lag)(lambda: forward(turn - lag))
        return carry

    lax.fori_loop(0, turns, pack_and_forward, 0)

    pair = iota((span * 16, 1), 0)
    slot_base = ((my_place // CORES) * sum(caps) + my_core * caps[0] + pair // 16) * 4
    lead = ((slot_base + pair // 4 % 4) * 2).astype(F32)
    tail = ((slot_base + pair % 4) * 2).astype(F32)
    c_tile = (c_row // 2).astype(F32)

    def describe(unit):
        tile, atom, col, quarter, valid = (jnp.zeros((span * 16, 1), F32) for _ in range(5))
        for q in range(4):
            hit = units[q] == unit
            tile = tile + lane_sum(jnp.where(hit, c_tile, 0.0))
            atom = atom + lane_sum(jnp.where(hit, c_atom.astype(F32), 0.0))
            col = col + lane_sum(jnp.where(hit, c_col, 0.0))
            count = lane_sum(jnp.where(hit, 1.0, 0.0))
            quarter = quarter + q * count
            valid = valid + count
        row_half = jnp.where(quarter > 1.5, 1.0, 0.0)
        return tile, atom, col, row_half, quarter - 2.0 * row_half, valid

    tile_a, atom_a, col_a, mh_a, nh_a, valid_a = describe(lead)
    tile_b, _, _, mh_b, nh_b, valid_b = describe(tail)
    joined = (tile_a == tile_b) & (valid_a > 0.5) & (valid_b > 0.5)
    index1 = jnp.where(joined & (nh_a == nh_b), atom_a * 16.0 + 4.0 * mh_b, -99.0)
    index2 = jnp.where(joined & (mh_a == mh_b), col_a * 16.0 + 8.0 + 4.0 * nh_a, -99.0)
    wait_bytes(table.at[pl.ds(0, n_far)], table_sem.at[1])
    greens = table[...].reshape(n_ao * 16, 128)
    g_row = iota((span * 16, n_ao * 16), 1)
    g_spot = g_row // 16
    g_atom = device(g_spot // n_y % n_x, g_spot % n_y, g_spot // (n_x * n_y))
    g_lane = (g_atom * 16 + g_row % 16).astype(F32)
    for target, index, half in ((v1, index1, mh_a), (v2, index2, nh_b)):
        rows = [dot(ones_where(g_lane == index + i), greens).astype(BF16) for i in range(4)]
        rows = dot(jnp.concatenate(rows, axis=1), mover)
        target[...] = jnp.where(half < 0.5, rows[:, :QUART], rows[:, QUART:])

    r, s = iota((QUART, QUART), 0), iota((QUART, QUART), 1)
    hi, lo = r // 16, r % 16
    spread1, gather1, keep1 = ones_where(hi == s % 16), ones_where(hi == s // 16), ones_where(lo == s % 16)
    spread2, gather2, keep2 = ones_where(lo == s // 16), ones_where(lo == s % 16), ones_where(hi == s // 16)

    def weights(j):
        for m in range(2):
            for a in range(2):
                for b in range(2):
                    rows, lanes = slice(a * QUART, (a + 1) * QUART), slice(b * QUART, (b + 1) * QUART)
                    vec = v1[pl.ds(j * 16 + (2 * m + a) * 4 + 2 * m + b, 1), :].astype(BF16)
                    w1[j, m, rows, lanes] = dot(spread1 * vec, gather1).astype(BF16) * keep1
                    vec = v2[pl.ds(j * 16 + (2 * a + m) * 4 + 2 * b + m, 1), :].astype(BF16)
                    w2[j, m, rows, lanes] = dot(spread2 * vec, gather2).astype(BF16) * keep2

    o, i = iota((n_y * 16, n_y * 16), 0), iota((n_y * 16, n_y * 16), 1)
    went = (i // 8 % 2 * 4 + i % 4) * (2 * n_y) + (i // 16) * 2 + i // 4 % 2
    sorter = ones_where(o == went)

    def unpack(source, turn, target):
        grp = origin(turn)
        block = source[pl.ds(grp * n_y, n_y)].reshape(n_y * 16, span * HALF)
        placed = dot(sorter, block).astype(BF16)
        rows = pl.ds(pl.multiple_of(grp * (2 * n_y), 2 * n_y), 2 * n_y)
        for h in range(2):
            for b in range(4):
                part = placed[(h * 4 + b) * 2 * n_y:(h * 4 + b + 1) * 2 * n_y]
                for j in range(span):
                    target[j, rows, b * QUART + h * HALF:b * QUART + (h + 1) * HALF] = part[:, j * HALF:(j + 1) * HALF]

    def contract(tiles, j):
        half = [dot(tiles[:, m * 512:(m + 1) * 512], w1[j, m]).astype(BF16) for m in range(2)]
        done = []
        for m in range(2):
            lanes = slice(m * QUART, (m + 1) * QUART)
            done.append(dot(jnp.concatenate([part[:, lanes] for part in half], axis=1), w2[j, m]).astype(BF16))
        return jnp.concatenate([done[m][:, a * QUART:(a + 1) * QUART] for a in range(2) for m in range(2)], axis=1)

    def weights_and_forward(j, carry):
        weights(j)
        for turn in range(turns - lag, turns):
            pl.when(j == (turn - turns + lag) * span // lag)(functools.partial(forward, turn))
        return carry

    lax.fori_loop(0, span, weights_and_forward, 0)

    def arrive(turn, carry):
        unpack(recv, turn, masked)
        return carry

    lax.fori_loop(0, turns, arrive, 0)

    same[...] = jnp.zeros_like(same)

    q, p = iota((n_p, n_p), 0), iota((n_p, n_p), 1)
    straight = ones_where(place(q // (4 * n_y), q // 4 % n_y, q // 2 % 2) * 2 + q % 2 == p)

    def own_slot(j, carry):
        tiles = masked[j]
        ordered = dot(straight, tiles).astype(BF16)
        same[...] += dot_nt(contract(tiles, j), ordered)
        masked[j] = ordered
        return carry

    lax.fori_loop(0, span, own_slot, 0)

    def scatter(c, part):
        for e in range(2):
            rs[c, :, e, :] = part[pl.ds(e, n_ao, stride=2), :]
        rs_in[c, pl.ds(my_place, 1)] = rs[c, pl.ds(my_place, 1)]

        def one(step, carry):
            peer = lax.rem(me + step, n_ao)
            at = place(peer // n_grp, peer // CORES % n_y, peer % CORES)
            pltpu.make_async_remote_copy(
                src_ref=rs.at[c, at], dst_ref=rs_in.at[c, my_place], send_sem=rs_sem.at[c], recv_sem=rs_sem.at[2 + c],
                device_id=(zz, peer), device_id_type=MESH,
            ).start()
            return carry

        lax.fori_loop(1, n_ao, one, 0, unroll=7)

    def gather(c):
        wait_bytes(rs_in.at[c, pl.ds(0, n_ao - 1)], rs_sem.at[2 + c])
        out_ref[c] = jnp.sum(rs_in[c], axis=0)

    scatter(0, same)

    def arrive_up(turn, carry):
        def act(c, count):
            wait_bytes(zup.at[pl.ds(origin(turn) * n_y, n_y), :, pl.ds(0, count * HALF)], zu_sem.at[turn])

        by_core(my_core, act)
        unpack(zup, turn, masked_up)
        return carry

    lax.fori_loop(0, turns, arrive_up, 0)
    cross[...] = jnp.zeros_like(cross)

    def up_slot(j, carry):
        cross[...] += dot_nt(contract(masked_up[j], j), masked[j])
        return carry

    lax.fori_loop(0, span, up_slot, 0)
    scatter(1, cross)
    gather(0)
    gather(1)

    wait_bytes(meta.at[pl.ds(0, n_ao - 1)], small_send.at[0])
    wait_bytes(table.at[pl.ds(0, n_y - 1)], small_send.at[1])
    wait_bytes(table.at[pl.ds(0, n_far)], small_send.at[2])
    if caps[0] == caps[1]:
        wait_bytes(send.at[pl.ds(0, n_ao - 1)], send_sem.at[0])
    else:
        for c in range(CORES):
            lanes = pl.ds(0, caps[c] * HALF)

            @pl.when(my_core == c)
            def _():
                wait_bytes(send.at[pl.ds(0, n_ao // CORES - 1), :, lanes], send_sem.at[c])

            @pl.when(my_core != c)
            def _():
                wait_bytes(send.at[pl.ds(0, n_ao // CORES), :, lanes], send_sem.at[c])

    def sent_up(c, count):
        wait_bytes(zup.at[:, :, pl.ds(0, count * HALF)], zs_sem)

    by_core(my_core, sent_up)
    for c in range(2):
        wait_bytes(rs.at[c, pl.ds(0, n_ao - 1)], rs_sem.at[c])


def run(caps, shape, ident, b_source, pair_cols, live_slots, g_occ, g_virt, atom_sizes):
    n_x, n_y, n_z = shape
    n_ao = n_x * n_y * CORES
    n_c, n_p = n_ao * SLOTS * 2, 2 * n_ao
    span = max(caps)
    vmem = pl.BlockSpec(memory_space=pltpu.VMEM)
    dma = pltpu.SemaphoreType.DMA
    return pl.pallas_call(
        functools.partial(kernel, (caps, n_x, n_y, n_z)),
        out_shape=(jax.ShapeDtypeStruct((2, 2, n_p), F32), jax.ShapeDtypeStruct((1, 1), jnp.int32)),
        in_specs=[pl.BlockSpec(memory_space=pl.ANY)] + [vmem] * 5,
        out_specs=(vmem, vmem),
        scratch_shapes=[
            pltpu.VMEM((n_ao, SLOTS, 2, TILE), BF16),
            pltpu.VMEM((4, n_c, QUART), BF16),
            pltpu.VMEM((n_ao, 1, 128), F32),
            pltpu.VMEM((n_ao, 16, 128), BF16),
            pltpu.VMEM((n_ao, 16, span * HALF), BF16),
            pltpu.VMEM((n_ao, 16, span * HALF), BF16),
            pltpu.VMEM((n_ao, 16, span * HALF), BF16),
            pltpu.VMEM((span, n_p, TILE), BF16),
            pltpu.VMEM((span, n_p, TILE), BF16),
            pltpu.VMEM((span, 2, 512, 512), BF16),
            pltpu.VMEM((span, 2, 512, 512), BF16),
            pltpu.VMEM((span * 16, QUART), F32),
            pltpu.VMEM((span * 16, QUART), F32),
            pltpu.VMEM((n_p, n_p), F32),
            pltpu.VMEM((n_p, n_p), F32),
            pltpu.VMEM((2, n_ao, 2, n_p), F32),
            pltpu.VMEM((2, n_ao, 2, n_p), F32),
            dma, dma, dma((2,)), dma((3,)), dma((2,)), dma((n_x * n_y,)), dma, dma((2 * n_x,)), dma((4,)),
        ],
        compiler_params=pltpu.CompilerParams(
            collective_id=ident, has_side_effects=True, vmem_limit_bytes=56 * 1024 * 1024
        ),
        name=f"blocks_{sum(caps)}",
    )(b_source, pair_cols, live_slots, g_occ, g_virt, atom_sizes)


def whole(shape, values):
    return run((8, 8), shape, 1, *values)[0]


def local(shape, b_source, g_occ, g_virt, atom_sizes, pair_cols, live_slots):
    given = (b_source, pair_cols, live_slots.reshape(1, 1), g_occ, g_virt, atom_sizes.reshape(1, -1))
    short, flag = run((4, 3), shape, 0, *given)
    return lax.cond(
        flag[0, 0] > 0, lambda *values: whole(shape, values), lambda *values: short, *given
    )


def solution(mesh):
    n_ao, n_z = mesh.shape["ao"], mesh.shape["aux"]
    n_x = 4 if n_ao >= 64 else 2
    return jax.shard_map(
        functools.partial(local, (n_x, n_ao // (n_x * CORES), n_z)),
        mesh=mesh,
        in_specs=(
            P(None, None, ("aux", "ao"), None),
            P("ao", None),
            P("ao", None),
            P(),
            P("ao", None),
            P("ao"),
        ),
        out_specs=P(None, ("aux", "ao"), None),
        check_vma=False,
    )
```
